32 devices in a mesh: dp: 2 (over x), ctx: 16 (over z, y, core).
Axes of the slice: x: 2, y: 2, z: 4, core: 2. Of those that a mesh axis runs over, the one named last changes fastest.
Arguments:
- hidden_in: bfloat16 [2, 2048, 2048], P('dp', 'ctx'), may hold values from -6 to 6
- qk_weight: bfloat16 [2048, 256], replicated, may hold values from -0.125 to 0.125
- conv_weight: float32 [3, 256], replicated, may hold values from -3 to 3
- values: bfloat16 [2, 2048, 512], P('dp', 'ctx'), may hold values from -6 to 6
- gate_in: bfloat16 [2, 2048, 512], P('dp', 'ctx'), may hold values from -6 to 6
- cotangent: bfloat16 [2, 2048, 512], P('dp', 'ctx'), may hold values from -6 to 6
Outputs:
- output: bfloat16 [2, 2048, 512], P('dp', 'ctx')
- grad_hidden: bfloat16 [2, 2048, 2048], P('dp', 'ctx')
- grad_values: bfloat16 [2, 2048, 512], P('dp', 'ctx')
- grad_gate: bfloat16 [2, 2048, 512], P('dp', 'ctx')
- grad_qk_weight: bfloat16 [2048, 256], replicated
The draws below stay inside these ranges and needn't reach their ends.
All inputs are finite; a program needn't handle non-finite values.
Results may differ from the reference program's by a relative error of at most 0.008.
Values may be sent and summed in bfloat16 or wider, within the bound.
A program may use at most 192 MiB of HBM per device.

```python
import math
import jax
import jax.numpy as jnp
import numpy as np
from jax import lax

D = 2048
H = 8
F = 16
DV = 64
FT = 153
KCONV = 3
TOK_DEV = 128
SEQS = 2
LEN = 2048


def shard_levels(key, shape, split, least, high):
    def one(position, shards_of):
        steps = jax.random.uniform(jax.random.fold_in(jax.random.fold_in(key, 6), position), (shards_of,), jnp.float32, least / len(split), high / len(split))
        return jnp.repeat(jnp.exp(steps), shape[position] // shards_of).reshape((-1,) + (1,) * (len(shape) - position - 1))

    loudness = one(*split[0])
    for cut in split[1:]:
        loudness = loudness * one(*cut)
    return loudness


def bell_draw(rng, dims, spread, limit, pieces=(), held_as=jnp.bfloat16):
    level = shard_levels(rng, dims, pieces, -0.22, 0.18) if pieces else 1.0
    values = jax.random.normal(rng, dims, jnp.float32) * spread * level
    return jnp.minimum(jnp.maximum(values, -limit), limit).astype(held_as)


def setup_inputs(seed: int = 0) -> dict:
    streams_of = jax.random.split(jax.random.key(seed), 7)
    return {
        "hidden_in": bell_draw(streams_of[0], (SEQS, LEN, D), 1.0, 6.0, ((0, 2), (1, 16))),
        "qk_weight": bell_draw(streams_of[1], (D, 2 * H * F), D ** -0.5, 0.125),
        "conv_weight": bell_draw(streams_of[2], (KCONV, 2 * H * F), 0.6, 3.0, (), jnp.float32),
        "values": bell_draw(streams_of[3], (SEQS, LEN, H * DV), 1.0, 6.0, ((0, 2), (1, 16))),
        "gate_in": bell_draw(streams_of[4], (SEQS, LEN, H * DV), 1.0, 6.0, ((0, 2), (1, 16))),
        "cotangent": bell_draw(streams_of[5], (SEQS, LEN, H * DV), 1.0, 6.0, ((0, 2), (1, 16))),
    }


def pair_table(feat_width):
    table = np.zeros((feat_width * feat_width, feat_width * (feat_width + 1) // 2), np.float32)
    column = 0
    for first in range(feat_width):
        for second in range(first, feat_width):
            factor = 1.0 / math.sqrt(feat_width)
            if first == second:
                factor = factor / math.sqrt(2.0)
            table[first * feat_width + second, column] = factor
            column += 1
    return table

def taylor_map(matrix):
    feat_width = matrix.shape[-1]
    outer = (matrix[..., :, None] * matrix[..., None, :]).reshape(matrix.shape[:-1] + (feat_width * feat_width,))
    second = jnp.dot(outer, pair_table(feat_width), precision=lax.Precision.HIGHEST)
    ones = jnp.ones(matrix.shape[:-1] + (1,), matrix.dtype)
    return jnp.concatenate([ones, matrix * feat_width ** (-0.25), second], -1)

def kernel_weights(queries, keys_mat):
    length = queries.shape[0]
    scores = jnp.einsum('thf,shf->hts', queries, keys_mat, precision=lax.Precision.HIGHEST) * queries.shape[-1] ** (-0.5)
    rows_idx = lax.broadcasted_iota(jnp.int32, (length, length), 0)
    cols_idx = lax.broadcasted_iota(jnp.int32, (length, length), 1)
    causal = rows_idx >= cols_idx
    return jnp.where(causal[None], 1.0 + scores + 0.5 * scores * scores, 0.0)

def block_out(queries, keys_mat, value_matrix, incoming_numerator, norm_in):
    weights_mat = kernel_weights(queries, keys_mat)
    query_feature_rows = taylor_map(queries)
    numerator = jnp.einsum('hts,shd->thd', weights_mat, value_matrix, precision=lax.Precision.HIGHEST)
    numerator = numerator + jnp.einsum('jfn,fna->jfa', query_feature_rows, incoming_numerator, precision=lax.Precision.HIGHEST)
    denom = lax.optimization_barrier(jnp.sum(weights_mat, 2)).T + jnp.einsum('thm,hm->th', query_feature_rows, norm_in, precision=lax.Precision.HIGHEST)
    return numerator / denom[..., None]

def block_state(keys_mat, value_matrix):
    key_feature_rows = taylor_map(keys_mat)
    return (jnp.einsum('oxa,oxn->xan', key_feature_rows, value_matrix, precision=lax.Precision.HIGHEST), lax.optimization_barrier(jnp.sum(key_feature_rows, 0)))

def attention_core(queries, keys_mat, value_matrix):
    total = queries.shape[0]
    blocks = total // TOK_DEV
    query_blocks = queries.reshape(blocks, TOK_DEV, H, F)
    key_blocks = keys_mat.reshape(blocks, TOK_DEV, H, F)
    value_blocks = value_matrix.reshape(blocks, TOK_DEV, H, DV)
    start = (jnp.zeros((H, FT, DV), queries.dtype), jnp.zeros((H, FT), queries.dtype))

    def advance(carry, block):
        incoming_numerator, norm_in = carry
        query_b, key_b, value_b = block
        result = block_out(query_b, key_b, value_b, incoming_numerator, norm_in)
        numer_new, norm_new = block_state(key_b, value_b)
        return ((incoming_numerator + numer_new, norm_in + norm_new), result)
    unused, results = lax.scan(advance, start, (query_blocks, key_blocks, value_blocks))
    return results.reshape(total, H, DV)

def short_conv(projected, conv_weight):
    length = projected.shape[0]
    padded = jnp.concatenate([jnp.zeros((KCONV - 1, projected.shape[1]), projected.dtype), projected], 0)
    total = conv_weight[0] * padded[KCONV - 1:KCONV - 1 + length]
    for offset in range(1, KCONV):
        total = total + conv_weight[offset] * padded[KCONV - 1 - offset:KCONV - 1 - offset + length]
    return total

def short_conv_back(grads, conv_weight):
    length = grads.shape[0]
    padded = jnp.concatenate([grads, jnp.zeros((KCONV - 1, grads.shape[1]), grads.dtype)], 0)
    total = conv_weight[0] * padded[0:length]
    for offset in range(1, KCONV):
        total = total + conv_weight[offset] * padded[offset:offset + length]
    return total

def reference(hidden_in, qk_weight, conv_weight, values, gate_in, cotangent):
    outputs = []
    grads_hidden = []
    grads_value = []
    grads_gate = []
    weight_total = jnp.zeros((D, 2 * H * F), jnp.float32)
    for seq in range(SEQS):
        tokens = hidden_in[seq]
        projected = jnp.dot(tokens, qk_weight, preferred_element_type=jnp.float32).astype(jnp.bfloat16)
        mixed = short_conv(projected.astype(jnp.float32), conv_weight)
        queries = mixed[:, :H * F].reshape(LEN, H, F)
        keys_mat = mixed[:, H * F:].reshape(LEN, H, F)
        value_matrix = values[seq].astype(jnp.float32).reshape(LEN, H, DV)
        attended, pull = jax.vjp(attention_core, queries, keys_mat, value_matrix)
        attended = attended.reshape(LEN, H * DV)
        gate_f = gate_in[seq].astype(jnp.float32)
        sigm = jax.nn.sigmoid(gate_f)
        gate_act = gate_f * sigm
        outputs.append((attended * gate_act).astype(jnp.bfloat16))
        upstream = cotangent[seq].astype(jnp.float32)
        grads_gate.append((upstream * attended * sigm * (1.0 + gate_f * (1.0 - sigm))).astype(jnp.bfloat16))
        grad_attended = (upstream * gate_act).reshape(LEN, H, DV)
        grad_query, grad_key, value_gradient_rows = pull(grad_attended)
        grads_value.append(value_gradient_rows.reshape(LEN, H * DV).astype(jnp.bfloat16))
        grad_mixed = jnp.concatenate([grad_query.reshape(LEN, H * F), grad_key.reshape(LEN, H * F)], 1)
        grad_projected = short_conv_back(grad_mixed, conv_weight).astype(jnp.bfloat16)
        grads_hidden.append(jnp.dot(grad_projected, qk_weight.T, preferred_element_type=jnp.float32).astype(jnp.bfloat16))
        weight_total = weight_total + jnp.dot(tokens.T, grad_projected, preferred_element_type=jnp.float32)
    return (jnp.stack(outputs), jnp.stack(grads_hidden), jnp.stack(grads_value), jnp.stack(grads_gate), weight_total.astype(jnp.bfloat16))
```

```python
import functools

import jax
import jax.numpy as jnp
import numpy as np
from jax import lax
from jax.experimental import pallas as pl
from jax.experimental.pallas import tpu as pltpu
from jax.sharding import PartitionSpec as P

H = 8
F = 16
DV = 64
KCONV = 3
FP = 256
F32 = jnp.float32
BF16 = jnp.bfloat16
MESH = pl.DeviceIdType.MESH
VM = pl.BlockSpec(memory_space=pltpu.VMEM)
NORM_ROW = H * DV + 2 * DV


def feature_tables():
    pairs = [(a, b) for a in range(F + 1) for b in range(a, F + 1)]
    first = np.zeros((H * F, H * FP), np.float32)
    second = np.zeros((H * F, H * FP), np.float32)
    rows = np.zeros((8, H * FP), np.float32)
    for h in range(H):
        for m, (a, b) in enumerate(pairs):
            lane = h * FP + (m if m < 128 else 128 + 32 * (h % 4) + m - 128)
            if a:
                first[h * F + a - 1, lane] = 1.0
            else:
                rows[0, lane] = 1.0
            if b:
                second[h * F + b - 1, lane] = 1.0
            else:
                rows[1, lane] = 1.0
            scale = 1.0 if b == 0 else 1.0 / F**0.5 if a == 0 else 1.0 / F
            rows[2, lane] = scale * (0.5 if a == b and a else 1.0)
    return first, second, rows


def mm(a, b, ca=1, cb=0):
    return lax.dot_general(a, b, (((ca,), (cb,)), ((), ())), preferred_element_type=F32)


def head_slice(array, h):
    return array[:, h * DV : (h + 1) * DV]


def head_state(state, h):
    tail = H * DV + (h // 4) * DV
    return jnp.concatenate(
        [state[h * DV : (h + 1) * DV], state[tail : tail + DV]], 1
    )


def head_norm(norms, h):
    tail = H + h // 4
    return jnp.concatenate([norms[h : h + 1], norms[tail : tail + 1]], 1)


def store_state(ref, states, norms):
    for h in range(H):
        ref[h * DV : (h + 1) * DV, :] = states[h][:, :128].astype(BF16)
    for g in range(2):
        tail = sum(states[4 * g + i][:, 128:] for i in range(4))
        ref[H * DV + g * DV : H * DV + (g + 1) * DV, :] = tail.astype(BF16)
    rows = [norms[h][:, :128] for h in range(H)]
    rows += [sum(norms[4 * g + i][:, 128:] for i in range(4)) for g in range(2)]
    rows.append(jnp.zeros((16 - len(rows), 128), F32))
    ref[NORM_ROW : NORM_ROW + 16, :] = jnp.concatenate(rows, 0).astype(BF16)
    rest = ref.shape[0] - NORM_ROW - 16
    if rest:
        ref[NORM_ROW + 16 :, :] = jnp.zeros((rest, 128), BF16)


def key_kernel(proj, prev, conv, values, first, second, rows, mixed_out, state_out):
    length = proj.shape[0]
    padded = jnp.concatenate([prev[...], proj[...].astype(F32)], 0)
    mixed = conv[0:1, :] * padded[8 : 8 + length]
    for j in range(1, KCONV):
        mixed = mixed + conv[j : j + 1, :] * padded[8 - j : 8 - j + length]
    mixed_out[...] = mixed
    keys = mixed[:, H * F :].astype(BF16)
    states, norms = [], []
    for h in range(H):
        at = slice(h * FP, (h + 1) * FP)
        phi = (mm(keys, first[:, at]) + rows[0:1, at]) * (mm(keys, second[:, at]) + rows[1:2, at])
        states.append(mm(head_slice(values, h), phi.astype(BF16), 0, 0))
        norms.append(jnp.sum(phi, 0, keepdims=True))
    store_state(state_out, states, norms)


def query_kernel(
    mixed, values, gate, cot, state, first, second, rows, out, ggate, state_out, dq_out, dk_out, dv_out
):
    length = mixed.shape[0]
    q = mixed[:, : H * F].astype(BF16)
    k = mixed[:, H * F :].astype(BF16)
    lane = lax.broadcasted_iota(jnp.int32, (length, H * F), 1) // F
    causal = lax.broadcasted_iota(jnp.int32, (length, length), 0) >= lax.broadcasted_iota(
        jnp.int32, (length, length), 1
    )
    zero = jnp.zeros_like(q)
    incoming = state[...]
    norm_rows = incoming[NORM_ROW : NORM_ROW + 16].astype(F32)
    dq = jnp.zeros((length, H * F), F32)
    dk = jnp.zeros((length, H * F), F32)
    states, norms, outs, ggates, dvs = [], [], [], [], []
    for h in range(H):
        at = slice(h * FP, (h + 1) * FP)
        first_h, second_h, scale = first[:, at], second[:, at], rows[2:3, at]
        qh = jnp.where(lane == h, q, zero)
        kh = jnp.where(lane == h, k, zero)
        v = head_slice(values, h)
        s = mm(qh, k, 1, 1) * F**-0.5
        w = jnp.where(causal, 1.0 + s + 0.5 * s * s, 0.0)
        w16 = w.astype(BF16)
        one = mm(q, first_h) + rows[0:1, at]
        two = (mm(q, second_h) + rows[1:2, at]) * scale
        phi = one * two
        phi16 = phi.astype(BF16)
        state_h = head_state(incoming, h)
        norm_h = head_norm(norm_rows, h)
        den = jnp.sum(w, 1, keepdims=True) + jnp.sum(phi * norm_h, 1, keepdims=True)
        inv = 1.0 / den
        att = (mm(w16, v) + mm(phi16, state_h, 1, 1)) * inv
        g = head_slice(gate, h).astype(F32)
        up = head_slice(cot, h).astype(F32)
        sig = 1.0 / (1.0 + jnp.exp(-g))
        act = g * sig
        ga = up * act
        gd = -jnp.sum(ga * att, 1, keepdims=True) * inv
        ng = (ga * inv).astype(BF16)
        outs.append((att * act).astype(BF16))
        ggates.append((up * att * sig * (1.0 + g * (1.0 - sig))).astype(BF16))
        states.append(mm(ng, phi16, 0, 0))
        norms.append(jnp.sum(gd * phi, 0, keepdims=True))
        dw = mm(ng, v, 1, 1) + gd
        ds = (jnp.where(causal, dw * (1.0 + s), 0.0) * F**-0.5).astype(BF16)
        dphi = mm(ng, state_h) + gd * norm_h
        dq = dq + mm(ds, kh)
        dq = dq + mm((dphi * two).astype(BF16), first_h, 1, 1)
        dq = dq + mm((dphi * one * scale).astype(BF16), second_h, 1, 1)
        dk = dk + mm(ds, qh, 0, 0)
        dvs.append(mm(w16, ng, 0, 0))
    for p in range(H // 2):
        at = slice(2 * p * DV, 2 * (p + 1) * DV)
        out[:, at] = jnp.concatenate(outs[2 * p : 2 * p + 2], 1)
        ggate[:, at] = jnp.concatenate(ggates[2 * p : 2 * p + 2], 1)
        dv_out[:, at] = jnp.concatenate(dvs[2 * p : 2 * p + 2], 1)
    store_state(state_out, states, norms)
    dq_out[...] = dq
    dk_out[...] = dk


def value_kernel(mixed, values, state, dq_in, dk_in, dv_in, first, second, rows, gv, gm):
    keys = mixed[:, H * F :].astype(BF16)
    incoming = state[...]
    norm_rows = incoming[NORM_ROW : NORM_ROW + 16].astype(F32)
    dk = dk_in[...]
    dvs = []
    for h in range(H):
        at = slice(h * FP, (h + 1) * FP)
        first_h, second_h = first[:, at], second[:, at]
        one = mm(keys, first_h) + rows[0:1, at]
        two = mm(keys, second_h) + rows[1:2, at]
        state_h = head_state(incoming, h)
        dphi = mm(head_slice(values, h), state_h) + head_norm(norm_rows, h)
        dk = dk + mm((dphi * two).astype(BF16), first_h, 1, 1)
        dk = dk + mm((dphi * one).astype(BF16), second_h, 1, 1)
        dvs.append(mm((one * two).astype(BF16), state_h, 1, 1))
    for p in range(H // 2):
        at = slice(2 * p * DV, 2 * (p + 1) * DV)
        gv[:, at] = (dv_in[:, at] + jnp.concatenate(dvs[2 * p : 2 * p + 2], 1)).astype(BF16)
    gm[:, : H * F] = dq_in[...]
    gm[:, H * F :] = dk


def hidden_kernel(gm, later, conv, weight, gp_out, gh):
    length = gm.shape[0]
    extended = jnp.concatenate([gm[...], later[...]], 0)
    gp = conv[0:1, :] * extended[0:length]
    for j in range(1, KCONV):
        gp = gp + conv[j : j + 1, :] * extended[j : j + length]
    gp = gp.astype(BF16)
    gp_out[...] = gp
    gh[...] = mm(gp, weight[...], 1, 1).astype(BF16)


def scan_kernel(n, backward, state, out, got, sums, send1, recv1, send2, recv2):
    me = lax.axis_index("ctx")
    dp = lax.axis_index("dp")

    def peer(off):
        return lax.rem(me + off, n)

    barrier = pltpu.get_barrier_semaphore()

    def greet(off, c):
        pl.semaphore_signal(barrier, inc=1, device_id=(dp, peer(off)), device_id_type=MESH)
        return c

    lax.fori_loop(1, n, greet, 0)
    pl.semaphore_wait(barrier, n - 1)

    def copy1(off):
        return pltpu.make_async_remote_copy(
            src_ref=state.at[peer(off)], dst_ref=got.at[me], send_sem=send1.at[off],
            recv_sem=recv1.at[off], device_id=(dp, peer(off)), device_id_type=MESH,
        )

    def copy2(off):
        return pltpu.make_async_remote_copy(
            src_ref=sums.at[peer(off)], dst_ref=out.at[me], send_sem=send2.at[off],
            recv_sem=recv2.at[off], device_id=(dp, peer(off)), device_id_type=MESH,
        )

    def each(f):
        def step(off, c):
            f(off)
            return c
        lax.fori_loop(1, n, step, 0)

    each(lambda off: copy1(off).start())
    got[me] = state[me]
    each(lambda off: copy1(off).wait_recv())

    def add(i, total):
        at = n - 1 - i if backward else i
        sums[at] = total.astype(BF16)
        return total + got[at].astype(F32)

    lax.fori_loop(0, n, add, jnp.zeros(got.shape[1:], F32))
    each(lambda off: copy2(off).start())
    out[me] = sums[me]
    each(lambda off: copy2(off).wait_recv())
    each(lambda off: copy1(off).wait_send())
    each(lambda off: copy2(off).wait_send())


def weight_kernel(n, dps, gp, hidden, out, gps, hid, part, got, sa, ra, sb, rb, sc, rc, sd, rd, se, re):
    dp, me = lax.axis_index("dp"), lax.axis_index("ctx")
    half = n // 2
    core, place = lax.rem(me, 2), me // 2
    own = dp * 2 + core
    team = dps * 2
    width = hidden.shape[1] // team
    tokens = hidden.shape[0]

    def member(i):
        return (i // 2, place * 2 + lax.rem(i, 2))

    def mate(off):
        return lax.rem(own + off, team)

    def peer(off):
        return lax.rem(place + off, half)

    barrier = pltpu.get_barrier_semaphore()

    def each(count, f):
        def step(off, c):
            f(off)
            return c
        lax.fori_loop(1, count, step, 0)

    def greet(device):
        pl.semaphore_signal(barrier, inc=1, device_id=device, device_id_type=MESH)

    each(team, lambda off: greet(member(mate(off))))
    each(half, lambda off: greet((dp, peer(off) * 2 + core)))
    pl.semaphore_wait(barrier, team + half - 2)

    def remote(src, dst, s, r, device):
        return pltpu.make_async_remote_copy(
            src_ref=src, dst_ref=dst, send_sem=s, recv_sem=r, device_id=device, device_id_type=MESH
        )

    def columns(i):
        return pl.ds(pl.multiple_of(i * width, width), width)

    def copy_gp(off):
        return remote(gp, gps.at[own], sa.at[off], ra.at[off], member(mate(off)))

    def copy_hid(off):
        return remote(
            hidden.at[:, columns(mate(off))], hid.at[own], sb.at[off], rb.at[off], member(mate(off))
        )

    def copy_part(off):
        return remote(
            part.at[peer(off)], got.at[place], sc.at[off], rc.at[off], (dp, peer(off) * 2 + core)
        )

    def copy_sum(off):
        return remote(
            out.at[own, place], out.at[own, place], sd.at[off], rd.at[off],
            (dp, peer(off) * 2 + core),
        )

    def copy_team(off):
        return remote(out.at[own], out.at[own], se.at[off], re.at[off], member(mate(off)))

    each(team, lambda off: copy_gp(off).start())
    each(team, lambda off: copy_hid(off).start())
    gps[own] = gp[...]
    hid[own] = hidden[:, columns(own)]
    each(team, lambda off: copy_gp(off).wait_recv())
    each(team, lambda off: copy_hid(off).wait_recv())
    total = mm(hid[0], gps[0], 0, 0)
    for i in range(1, team):
        total = total + mm(hid[i], gps[i], 0, 0)
    part[...] = total.reshape(part.shape).astype(BF16)
    each(half, lambda off: copy_part(off).start())
    got[place] = part[place]
    each(half, lambda off: copy_part(off).wait_recv())

    def add(i, total):
        return total + got[i].astype(F32)

    out[own, place] = lax.fori_loop(0, half, add, jnp.zeros(got.shape[1:], F32)).astype(BF16)
    each(half, lambda off: copy_sum(off).start())
    each(half, lambda off: copy_sum(off).wait_recv())
    each(half, lambda off: copy_sum(off).wait_send())
    each(team, lambda off: copy_team(off).start())
    each(team, lambda off: copy_team(off).wait_recv())
    each(team, lambda off: copy_team(off).wait_send())
    each(team, lambda off: copy_gp(off).wait_send())
    each(team, lambda off: copy_hid(off).wait_send())
    each(half, lambda off: copy_part(off).wait_send())


def call(kernel, ins, outs, scratch=(), collective=None):
    extra = {} if collective is None else dict(collective_id=collective, has_side_effects=True)
    return pl.pallas_call(
        kernel,
        out_shape=[jax.ShapeDtypeStruct(s, t) for s, t in outs],
        in_specs=[VM] * len(ins),
        out_specs=[VM] * len(outs),
        scratch_shapes=list(scratch),
        compiler_params=pltpu.CompilerParams(vmem_limit_bytes=48 * 2**20, **extra),
    )(*ins)


def scan(state, n, backward):
    slices = state.reshape(n, -1, 128)
    sems = [pltpu.SemaphoreType.DMA((n,))] * 4
    (out,) = call(
        functools.partial(scan_kernel, n, backward), [slices], [(slices.shape, BF16)],
        [pltpu.VMEM(slices.shape, BF16)] * 2 + sems, collective=1 if backward else 0,
    )
    return out.reshape(-1, 128)


def shifted(array, axis, by):
    length = lax.axis_size(axis)
    pairs = [(i, i + by) for i in range(length) if 0 <= i + by < length]
    return lax.ppermute(array, axis, pairs)


def body(n, dps, hidden_in, qk_weight, conv_weight, values, gate_in, cotangent):
    tokens, v, gate, cot = hidden_in[0], values[0], gate_in[0], cotangent[0]
    length, depth = tokens.shape
    cols = qk_weight.shape[1]
    wide = v.shape[1]
    first, second, rows = feature_tables()
    tables = [jnp.asarray(first, BF16), jnp.asarray(second, BF16), jnp.asarray(rows)]
    state_rows = n * 16 * -(-(NORM_ROW + 16) // (16 * n))
    state_shape = ((state_rows, 128), BF16)

    projected = jnp.dot(tokens, qk_weight, preferred_element_type=F32).astype(BF16)
    prev = shifted(projected[length - 8 :], "ctx", 1).astype(F32)
    mixed, own = call(
        key_kernel, [projected, prev, conv_weight, v, *tables], [((length, cols), F32), state_shape]
    )
    before = scan(own, n, False)
    out, ggate, own_grad, dq, dk, dv = call(
        query_kernel,
        [mixed, v, gate, cot, before, *tables],
        [
            ((length, wide), BF16), ((length, wide), BF16), state_shape,
            ((length, cols // 2), F32), ((length, cols // 2), F32), ((length, wide), F32),
        ],
    )
    after = scan(own_grad, n, True)
    gv, gm = call(
        value_kernel, [mixed, v, after, dq, dk, dv, *tables],
        [((length, wide), BF16), ((length, cols), F32)],
    )
    later = shifted(gm[:8], "ctx", -1)
    gp, gh = call(
        hidden_kernel, [gm, later, conv_weight, qk_weight],
        [((length, cols), BF16), ((length, depth), BF16)],
    )
    team, half = 2 * dps, n // 2
    piece = depth // (team * half)
    sem = pltpu.SemaphoreType.DMA
    (gw,) = call(
        functools.partial(weight_kernel, n, dps), [gp, tokens],
        [((team, half, piece, cols), BF16)],
        [
            pltpu.VMEM((team, length, cols), BF16),
            pltpu.VMEM((team, length, depth // team), BF16),
            pltpu.VMEM((half, piece, cols), BF16),
            pltpu.VMEM((half, piece, cols), BF16),
        ]
        + [sem((team,))] * 4 + [sem((half,))] * 4 + [sem((team,))] * 2,
        collective=2,
    )
    return out[None], gh[None], gv[None], ggate[None], gw.reshape(depth, cols)


def solution(mesh):
    split = P("dp", "ctx", None)
    return jax.shard_map(
        functools.partial(body, mesh.shape["ctx"], mesh.shape["dp"]),
        mesh=mesh,
        in_specs=(split, P(), P(), split, split, split),
        out_specs=(split, split, split, split, P()),
        check_vma=False,
    )
```

```python
import functools

import jax
import jax.numpy as jnp
import numpy as np
from jax import lax
from jax.experimental import pallas as pl
from jax.experimental.pallas import tpu as pltpu
from jax.sharding import PartitionSpec as P

H = 8
F = 16
DV = 64
KCONV = 3
FP = 256
F32 = jnp.float32
BF16 = jnp.bfloat16
MESH = pl.DeviceIdType.MESH
VM = pl.BlockSpec(memory_space=pltpu.VMEM)
NORM_ROW = H * DV + 2 * DV


def feature_tables():
    pairs = [(a, b) for a in range(F + 1) for b in range(a, F + 1)]
    first = np.zeros((H * F, H * FP), np.float32)
    second = np.zeros((H * F, H * FP), np.float32)
    rows = np.zeros((8, H * FP), np.float32)
    for h in range(H):
        for m, (a, b) in enumerate(pairs):
            lane = h * FP + (m if m < 128 else 128 + 32 * (h % 4) + m - 128)
            if a:
                first[h * F + a - 1, lane] = 1.0
            else:
                rows[0, lane] = 1.0
            if b:
                second[h * F + b - 1, lane] = 1.0
            else:
                rows[1, lane] = 1.0
            scale = 1.0 if b == 0 else 1.0 / F**0.5 if a == 0 else 1.0 / F
            rows[2, lane] = scale * (0.5 if a == b and a else 1.0)
    return first, second, rows


def mm(a, b, ca=1, cb=0):
    return lax.dot_general(a, b, (((ca,), (cb,)), ((), ())), preferred_element_type=F32)


def head_slice(array, h):
    return array[:, h * DV : (h + 1) * DV]


def head_state(state, h):
    tail = H * DV + (h // 4) * DV
    return jnp.concatenate(
        [state[h * DV : (h + 1) * DV], state[tail : tail + DV]], 1
    )


def head_norm(norms, h):
    tail = H + h // 4
    return jnp.concatenate([norms[h : h + 1], norms[tail : tail + 1]], 1)


def store_state(ref, states, norms):
    for h in range(H):
        ref[h * DV : (h + 1) * DV, :] = states[h][:, :128].astype(BF16)
    for g in range(2):
        tail = sum(states[4 * g + i][:, 128:] for i in range(4))
        ref[H * DV + g * DV : H * DV + (g + 1) * DV, :] = tail.astype(BF16)
    rows = [norms[h][:, :128] for h in range(H)]
    rows += [sum(norms[4 * g + i][:, 128:] for i in range(4)) for g in range(2)]
    rows.append(jnp.zeros((16 - len(rows), 128), F32))
    ref[NORM_ROW : NORM_ROW + 16, :] = jnp.concatenate(rows, 0).astype(BF16)
    rest = ref.shape[0] - NORM_ROW - 16
    if rest:
        ref[NORM_ROW + 16 :, :] = jnp.zeros((rest, 128), BF16)


def key_kernel(proj, prev, conv, values, first, second, rows, mixed_out, state_out):
    length = proj.shape[0]
    padded = jnp.concatenate([prev[...], proj[...].astype(F32)], 0)
    mixed = conv[0:1, :] * padded[8 : 8 + length]
    for j in range(1, KCONV):
        mixed = mixed + conv[j : j + 1, :] * padded[8 - j : 8 - j + length]
    mixed_out[...] = mixed
    keys = mixed[:, H * F :].astype(BF16)
    states, norms = [], []
    for h in range(H):
        at = slice(h * FP, (h + 1) * FP)
        phi = (mm(keys, first[:, at]) + rows[0:1, at]) * (mm(keys, second[:, at]) + rows[1:2, at])
        states.append(mm(head_slice(values, h), phi.astype(BF16), 0, 0))
        norms.append(jnp.sum(phi, 0, keepdims=True))
    store_state(state_out, states, norms)


def query_kernel(
    mixed, values, gate, cot, state, first, second, rows, out, ggate, state_out, dq_out, dk_out, dv_out
):
    length = mixed.shape[0]
    q = mixed[:, : H * F].astype(BF16)
    k = mixed[:, H * F :].astype(BF16)
    lane = lax.broadcasted_iota(jnp.int32, (length, H * F), 1) // F
    causal = lax.broadcasted_iota(jnp.int32, (length, length), 0) >= lax.broadcasted_iota(
        jnp.int32, (length, length), 1
    )
    zero = jnp.zeros_like(q)
    incoming = state[...]
    norm_rows = incoming[NORM_ROW : NORM_ROW + 16].astype(F32)
    dq = jnp.zeros((length, H * F), F32)
    dk = jnp.zeros((length, H * F), F32)
    states, norms, outs, ggates, dvs = [], [], [], [], []
    for h in range(H):
        at = slice(h * FP, (h + 1) * FP)
        first_h, second_h, scale = first[:, at], second[:, at], rows[2:3, at]
        qh = jnp.where(lane == h, q, zero)
        kh = jnp.where(lane == h, k, zero)
        v = head_slice(values, h)
        s = mm(qh, k, 1, 1) * F**-0.5
        w = jnp.where(causal, 1.0 + s + 0.5 * s * s, 0.0)
        w16 = w.astype(BF16)
        one = mm(q, first_h) + rows[0:1, at]
        two = (mm(q, second_h) + rows[1:2, at]) * scale
        phi = one * two
        phi16 = phi.astype(BF16)
        state_h = head_state(incoming, h)
        norm_h = head_norm(norm_rows, h)
        den = jnp.sum(w, 1, keepdims=True) + jnp.sum(phi * norm_h, 1, keepdims=True)
        inv = 1.0 / den
        att = (mm(w16, v) + mm(phi16, state_h, 1, 1)) * inv
        g = head_slice(gate, h).astype(F32)
        up = head_slice(cot, h).astype(F32)
        sig = 1.0 / (1.0 + jnp.exp(-g))
        act = g * sig
        ga = up * act
        gd = -jnp.sum(ga * att, 1, keepdims=True) * inv
        ng = (ga * inv).astype(BF16)
        outs.append((att * act).astype(BF16))
        ggates.append((up * att * sig * (1.0 + g * (1.0 - sig))).astype(BF16))
        states.append(mm(ng, phi16, 0, 0))
        norms.append(jnp.sum(gd * phi, 0, keepdims=True))
        dw = mm(ng, v, 1, 1) + gd
        ds = (jnp.where(causal, dw * (1.0 + s), 0.0) * F**-0.5).astype(BF16)
        dphi = mm(ng, state_h) + gd * norm_h
        dq = dq + mm(ds, kh)
        dq = dq + mm((dphi * two).astype(BF16), first_h, 1, 1)
        dq = dq + mm((dphi * one * scale).astype(BF16), second_h, 1, 1)
        dk = dk + mm(ds, qh, 0, 0)
        dvs.append(mm(w16, ng, 0, 0))
    for p in range(H // 2):
        at = slice(2 * p * DV, 2 * (p + 1) * DV)
        out[:, at] = jnp.concatenate(outs[2 * p : 2 * p + 2], 1)
        ggate[:, at] = jnp.concatenate(ggates[2 * p : 2 * p + 2], 1)
        dv_out[:, at] = jnp.concatenate(dvs[2 * p : 2 * p + 2], 1)
    store_state(state_out, states, norms)
    dq_out[...] = dq
    dk_out[...] = dk


def value_kernel(mixed, values, state, dq_in, dk_in, dv_in, first, second, rows, gv, gm):
    keys = mixed[:, H * F :].astype(BF16)
    incoming = state[...]
    norm_rows = incoming[NORM_ROW : NORM_ROW + 16].astype(F32)
    dk = dk_in[...]
    dvs = []
    for h in range(H):
        at = slice(h * FP, (h + 1) * FP)
        first_h, second_h = first[:, at], second[:, at]
        one = mm(keys, first_h) + rows[0:1, at]
        two = mm(keys, second_h) + rows[1:2, at]
        state_h = head_state(incoming, h)
        dphi = mm(head_slice(values, h), state_h) + head_norm(norm_rows, h)
        dk = dk + mm((dphi * two).astype(BF16), first_h, 1, 1)
        dk = dk + mm((dphi * one).astype(BF16), second_h, 1, 1)
        dvs.append(mm((one * two).astype(BF16), state_h, 1, 1))
    for p in range(H // 2):
        at = slice(2 * p * DV, 2 * (p + 1) * DV)
        gv[:, at] = (dv_in[:, at] + jnp.concatenate(dvs[2 * p : 2 * p + 2], 1)).astype(BF16)
    gm[:, : H * F] = dq_in[...]
    gm[:, H * F :] = dk


def hidden_kernel(gm, later, conv, weight, gp_out, gh):
    length = gm.shape[0]
    extended = jnp.concatenate([gm[...], later[...]], 0)
    gp = conv[0:1, :] * extended[0:length]
    for j in range(1, KCONV):
        gp = gp + conv[j : j + 1, :] * extended[j : j + length]
    gp = gp.astype(BF16)
    gp_out[...] = gp
    gh[...] = mm(gp, weight[...], 1, 1).astype(BF16)


def scan_kernel(n, dps, backward, *refs):
    if backward:
        state, out, got, sums, send1, recv1, send2, recv2 = refs
        team = 1
    else:
        state, hidden, out, hid, got, sums, send1, recv1, send2, recv2, send3, recv3 = refs
        team = 2 * dps
        width = hidden.shape[1] // team
    me = lax.axis_index("ctx")
    dp = lax.axis_index("dp")
    core, place = lax.rem(me, 2), me // 2
    mine = dp * 2 + core

    def peer(off):
        return lax.rem(me + off, n)

    barrier = pltpu.get_barrier_semaphore()

    def greet(off, c):
        pl.semaphore_signal(barrier, inc=1, device_id=(dp, peer(off)), device_id_type=MESH)
        return c

    def mate(off):
        return lax.rem(mine + off, team)

    def member(i):
        return (i // 2, place * 2 + lax.rem(i, 2))

    def columns(i):
        return pl.ds(pl.multiple_of(i * width, width), width)

    def copy3(off):
        return pltpu.make_async_remote_copy(
            src_ref=hidden.at[:, columns(mate(off))], dst_ref=hid.at[mine], send_sem=send3.at[off],
            recv_sem=recv3.at[off], device_id=member(mate(off)), device_id_type=MESH,
        )

    lax.fori_loop(1, n, greet, 0)
    for off in range(1, team):
        pl.semaphore_signal(barrier, inc=1, device_id=member(mate(off)), device_id_type=MESH)
    pl.semaphore_wait(barrier, n + team - 2)

    def copy1(off):
        return pltpu.make_async_remote_copy(
            src_ref=state.at[peer(off)], dst_ref=got.at[me], send_sem=send1.at[off],
            recv_sem=recv1.at[off], device_id=(dp, peer(off)), device_id_type=MESH,
        )

    def copy2(off):
        return pltpu.make_async_remote_copy(
            src_ref=sums.at[peer(off)], dst_ref=out.at[me], send_sem=send2.at[off],
            recv_sem=recv2.at[off], device_id=(dp, peer(off)), device_id_type=MESH,
        )

    def each(f):
        def step(off, c):
            f(off)
            return c
        lax.fori_loop(1, n, step, 0)

    each(lambda off: copy1(off).start())
    for off in range(1, team):
        copy3(off).start()
    if team > 1:
        hid[mine] = hidden[:, columns(mine)]
    got[me] = state[me]
    each(lambda off: copy1(off).wait_recv())

    def add(i, total):
        at = n - 1 - i if backward else i
        sums[at] = total.astype(BF16)
        return total + got[at].astype(F32)

    lax.fori_loop(0, n, add, jnp.zeros(got.shape[1:], F32))
    each(lambda off: copy2(off).start())
    out[me] = sums[me]
    each(lambda off: copy2(off).wait_recv())
    each(lambda off: copy1(off).wait_send())
    each(lambda off: copy2(off).wait_send())
    for off in range(1, team):
        copy3(off).wait()


def weight_kernel(n, dps, gp, hid, out, gps, part, got, sa, ra, sc, rc, sd, rd, sx, rx, sy, ry):
    dp, me = lax.axis_index("dp"), lax.axis_index("ctx")
    half = n // 2
    core, place = lax.rem(me, 2), me // 2
    own = dp * 2 + core
    team = dps * 2

    def member(i):
        return (i // 2, place * 2 + lax.rem(i, 2))

    def mate(off):
        return lax.rem(own + off, team)

    def peer(off):
        return lax.rem(place + off, half)

    def side(off):
        return lax.rem(dp + off, dps)

    def slot(off):
        return lax.rem(place + half - off, half)

    barrier = pltpu.get_barrier_semaphore()

    def each(count, f, least=1):
        def step(off, c):
            f(off)
            return c
        lax.fori_loop(least, count, step, 0)

    def greet(device):
        pl.semaphore_signal(barrier, inc=1, device_id=device, device_id_type=MESH)

    each(team, lambda off: greet(member(mate(off))))
    each(half, lambda off: greet((dp, peer(off) * 2 + core)))
    pl.semaphore_wait(barrier, team + half - 2)

    def remote(src, dst, s, r, device):
        return pltpu.make_async_remote_copy(
            src_ref=src, dst_ref=dst, send_sem=s, recv_sem=r, device_id=device, device_id_type=MESH
        )

    def copy_gp(off):
        return remote(gp, gps.at[own], sa.at[off], ra.at[off], member(mate(off)))

    def copy_part(off):
        return remote(
            part.at[peer(off)], got.at[place], sc.at[off], rc.at[off], (dp, peer(off) * 2 + core)
        )

    def copy_sum(off):
        return remote(
            out.at[own, place], out.at[own, place], sd.at[off], rd.at[off],
            (dp, peer(off) * 2 + core),
        )

    def copy_side(d, off):
        ref = out.at[own, slot(off)]
        return remote(ref, ref, sx.at[d, off], rx.at[d, off], (side(d), me))

    def copy_core(d, off):
        ref = out.at[side(d) * 2 + core, slot(off)]
        return remote(ref, ref, sy.at[d, off], ry.at[d, off], (dp, place * 2 + 1 - core))

    each(team, lambda off: copy_gp(off).start())
    gps[own] = gp[...]
    each(team, lambda off: copy_gp(off).wait_recv())
    total = mm(hid[0], gps[0], 0, 0)
    for i in range(1, team):
        total = total + mm(hid[i], gps[i], 0, 0)
    part[...] = total.reshape(part.shape).astype(BF16)
    each(half, lambda off: copy_part(off).start())
    got[place] = part[place]
    each(half, lambda off: copy_part(off).wait_recv())

    def add(i, total):
        return total + got[i].astype(F32)

    out[own, place] = lax.fori_loop(0, half, add, jnp.zeros(got.shape[1:], F32)).astype(BF16)
    each(half, lambda off: copy_sum(off).start())

    def hand_on(off):
        for d in range(1, dps):
            copy_side(d, off).start()
        copy_core(0, off).start()

    def take_side(off):
        for d in range(1, dps):
            copy_side(d, off).wait_recv()
            copy_core(d, off).start()

    hand_on(0)

    def arrive(off):
        copy_sum(off).wait_recv()
        hand_on(off)
        take_side(off - 1)

    each(half, arrive)
    take_side(half - 1)

    def finish(off):
        for d in range(dps):
            copy_core(d, off).wait_recv()

    def sent(off):
        for d in range(dps):
            copy_core(d, off).wait_send()
        for d in range(1, dps):
            copy_side(d, off).wait_send()

    each(half, finish, 0)
    each(half, sent, 0)
    each(half, lambda off: copy_sum(off).wait_send())
    each(team, lambda off: copy_gp(off).wait_send())
    each(half, lambda off: copy_part(off).wait_send())


def call(kernel, ins, outs, scratch=(), collective=None):
    extra = {} if collective is None else dict(collective_id=collective, has_side_effects=True)
    return pl.pallas_call(
        kernel,
        out_shape=[jax.ShapeDtypeStruct(s, t) for s, t in outs],
        in_specs=[VM] * len(ins),
        out_specs=[VM] * len(outs),
        scratch_shapes=list(scratch),
        compiler_params=pltpu.CompilerParams(vmem_limit_bytes=48 * 2**20, **extra),
    )(*ins)


def scan(state, n, dps, hidden=None):
    slices = state.reshape(n, -1, 128)
    ins, outs = [slices], [(slices.shape, BF16)]
    sems = [pltpu.SemaphoreType.DMA((n,))] * 4
    if hidden is not None:
        team = 2 * dps
        ins.append(hidden)
        outs.append(((team, hidden.shape[0], hidden.shape[1] // team), BF16))
        sems = sems + [pltpu.SemaphoreType.DMA((team,))] * 2
    out, *rest = call(
        functools.partial(scan_kernel, n, dps, hidden is None), ins, outs,
        [pltpu.VMEM(slices.shape, BF16)] * 2 + sems, collective=1 if hidden is None else 0,
    )
    return out.reshape(-1, 128), *rest


def shifted(array, axis, by):
    length = lax.axis_size(axis)
    pairs = [(i, i + by) for i in range(length) if 0 <= i + by < length]
    return lax.ppermute(array, axis, pairs)


def body(n, dps, hidden_in, qk_weight, conv_weight, values, gate_in, cotangent):
    tokens, v, gate, cot = hidden_in[0], values[0], gate_in[0], cotangent[0]
    length, depth = tokens.shape
    cols = qk_weight.shape[1]
    wide = v.shape[1]
    first, second, rows = feature_tables()
    tables = [jnp.asarray(first, BF16), jnp.asarray(second, BF16), jnp.asarray(rows)]
    state_rows = n * 16 * -(-(NORM_ROW + 16) // (16 * n))
    state_shape = ((state_rows, 128), BF16)

    projected = jnp.dot(tokens, qk_weight, preferred_element_type=F32).astype(BF16)
    prev = shifted(projected[length - 8 :], "ctx", 1).astype(F32)
    mixed, own = call(
        key_kernel, [projected, prev, conv_weight, v, *tables], [((length, cols), F32), state_shape]
    )
    before, hid = scan(own, n, dps, tokens)
    out, ggate, own_grad, dq, dk, dv = call(
        query_kernel,
        [mixed, v, gate, cot, before, *tables],
        [
            ((length, wide), BF16), ((length, wide), BF16), state_shape,
            ((length, cols // 2), F32), ((length, cols // 2), F32), ((length, wide), F32),
        ],
    )
    (after,) = scan(own_grad, n, dps)
    gv, gm = call(
        value_kernel, [mixed, v, after, dq, dk, dv, *tables],
        [((length, wide), BF16), ((length, cols), F32)],
    )
    later = shifted(gm[:8], "ctx", -1)
    gp, gh = call(
        hidden_kernel, [gm, later, conv_weight, qk_weight],
        [((length, cols), BF16), ((length, depth), BF16)],
    )
    team, half = 2 * dps, n // 2
    piece = depth // (team * half)
    sem = pltpu.SemaphoreType.DMA
    (gw,) = call(
        functools.partial(weight_kernel, n, dps), [gp, hid],
        [((team, half, piece, cols), BF16)],
        [
            pltpu.VMEM((team, length, cols), BF16),
            pltpu.VMEM((half, piece, cols), BF16),
            pltpu.VMEM((half, piece, cols), BF16),
        ]
        + [sem((team,))] * 2 + [sem((half,))] * 4 + [sem((dps, half))] * 4,
        collective=2,
    )
    return out[None], gh[None], gv[None], ggate[None], gw.reshape(depth, cols)


def solution(mesh):
    split = P("dp", "ctx", None)
    return jax.shard_map(
        functools.partial(body, mesh.shape["ctx"], mesh.shape["dp"]),
        mesh=mesh,
        in_specs=(split, P(), P(), split, split, split),
        out_specs=(split, split, split, split, P()),
        check_vma=False,
    )
```

```python
import functools

import jax
import jax.numpy as jnp
import numpy as np
from jax import lax
from jax.experimental import pallas as pl
from jax.experimental.pallas import tpu as pltpu
from jax.sharding import PartitionSpec as P

H = 8
F = 16
DV = 64
KCONV = 3
FP = 256
F32 = jnp.float32
BF16 = jnp.bfloat16
MESH = pl.DeviceIdType.MESH
VM = pl.BlockSpec(memory_space=pltpu.VMEM)
NORM_ROW = H * DV + 2 * DV


def feature_tables():
    pairs = [(a, b) for a in range(F + 1) for b in range(a, F + 1)]
    first = np.zeros((H * F, H * FP), np.float32)
    second = np.zeros((H * F, H * FP), np.float32)
    rows = np.zeros((8, H * FP), np.float32)
    for h in range(H):
        for m, (a, b) in enumerate(pairs):
            lane = h * FP + (m if m < 128 else 128 + 32 * (h % 4) + m - 128)
            if a:
                first[h * F + a - 1, lane] = 1.0
            else:
                rows[0, lane] = 1.0
            if b:
                second[h * F + b - 1, lane] = 1.0
            else:
                rows[1, lane] = 1.0
            scale = 1.0 if b == 0 else 1.0 / F**0.5 if a == 0 else 1.0 / F
            rows[2, lane] = scale * (0.5 if a == b and a else 1.0)
    return first, second, rows


def mm(a, b, ca=1, cb=0):
    return lax.dot_general(a, b, (((ca,), (cb,)), ((), ())), preferred_element_type=F32)


def head_slice(array, h):
    return array[:, h * DV : (h + 1) * DV]


def head_state(state, h):
    tail = H * DV + (h // 4) * DV
    return jnp.concatenate(
        [state[h * DV : (h + 1) * DV], state[tail : tail + DV]], 1
    )


def head_norm(norms, h):
    tail = H + h // 4
    return jnp.concatenate([norms[h : h + 1], norms[tail : tail + 1]], 1)


def store_state(ref, states, norms):
    for h in range(H):
        ref[h * DV : (h + 1) * DV, :] = states[h][:, :128].astype(BF16)
    for g in range(2):
        tail = sum(states[4 * g + i][:, 128:] for i in range(4))
        ref[H * DV + g * DV : H * DV + (g + 1) * DV, :] = tail.astype(BF16)
    rows = [norms[h][:, :128] for h in range(H)]
    rows += [sum(norms[4 * g + i][:, 128:] for i in range(4)) for g in range(2)]
    rows.append(jnp.zeros((16 - len(rows), 128), F32))
    ref[NORM_ROW : NORM_ROW + 16, :] = jnp.concatenate(rows, 0).astype(BF16)
    rest = ref.shape[0] - NORM_ROW - 16
    if rest:
        ref[NORM_ROW + 16 :, :] = jnp.zeros((rest, 128), BF16)


def key_kernel(proj, prev, conv, values, first, second, rows, mixed_out, state_out):
    length = proj.shape[0]
    padded = jnp.concatenate([prev[...], proj[...].astype(F32)], 0)
    mixed = conv[0:1, :] * padded[8 : 8 + length]
    for j in range(1, KCONV):
        mixed = mixed + conv[j : j + 1, :] * padded[8 - j : 8 - j + length]
    mixed_out[...] = mixed
    keys = mixed[:, H * F :].astype(BF16)
    states, norms = [], []
    for h in range(H):
        at = slice(h * FP, (h + 1) * FP)
        phi = (mm(keys, first[:, at]) + rows[0:1, at]) * (mm(keys, second[:, at]) + rows[1:2, at])
        states.append(mm(head_slice(values, h), phi.astype(BF16), 0, 0))
        norms.append(jnp.sum(phi, 0, keepdims=True))
    store_state(state_out, states, norms)


def query_kernel(
    mixed, values, gate, cot, state, first, second, rows, out, ggate, state_out, dq_out, dk_out, dv_out
):
    length = mixed.shape[0]
    q = mixed[:, : H * F].astype(BF16)
    k = mixed[:, H * F :].astype(BF16)
    lane = lax.broadcasted_iota(jnp.int32, (length, H * F), 1) // F
    causal = lax.broadcasted_iota(jnp.int32, (length, length), 0) >= lax.broadcasted_iota(
        jnp.int32, (length, length), 1
    )
    zero = jnp.zeros_like(q)
    incoming = state[...]
    norm_rows = incoming[NORM_ROW : NORM_ROW + 16].astype(F32)
    dq = jnp.zeros((length, H * F), F32)
    dk = jnp.zeros((length, H * F), F32)
    states, norms, outs, ggates, dvs = [], [], [], [], []
    for h in range(H):
        at = slice(h * FP, (h + 1) * FP)
        first_h, second_h, scale = first[:, at], second[:, at], rows[2:3, at]
        qh = jnp.where(lane == h, q, zero)
        kh = jnp.where(lane == h, k, zero)
        v = head_slice(values, h)
        s = mm(qh, k, 1, 1) * F**-0.5
        w = jnp.where(causal, 1.0 + s + 0.5 * s * s, 0.0)
        w16 = w.astype(BF16)
        one = mm(q, first_h) + rows[0:1, at]
        two = (mm(q, second_h) + rows[1:2, at]) * scale
        phi = one * two
        phi16 = phi.astype(BF16)
        state_h = head_state(incoming, h)
        norm_h = head_norm(norm_rows, h)
        den = jnp.sum(w, 1, keepdims=True) + jnp.sum(phi * norm_h, 1, keepdims=True)
        inv = 1.0 / den
        att = (mm(w16, v) + mm(phi16, state_h, 1, 1)) * inv
        g = head_slice(gate, h).astype(F32)
        up = head_slice(cot, h).astype(F32)
        sig = 1.0 / (1.0 + jnp.exp(-g))
        act = g * sig
        ga = up * act
        gd = -jnp.sum(ga * att, 1, keepdims=True) * inv
        ng = (ga * inv).astype(BF16)
        outs.append((att * act).astype(BF16))
        ggates.append((up * att * sig * (1.0 + g * (1.0 - sig))).astype(BF16))
        states.append(mm(ng, phi16, 0, 0))
        norms.append(jnp.sum(gd * phi, 0, keepdims=True))
        dw = mm(ng, v, 1, 1) + gd
        ds = (jnp.where(causal, dw * (1.0 + s), 0.0) * F**-0.5).astype(BF16)
        dphi = mm(ng, state_h) + gd * norm_h
        dq = dq + mm(ds, kh)
        dq = dq + mm((dphi * two).astype(BF16), first_h, 1, 1)
        dq = dq + mm((dphi * one * scale).astype(BF16), second_h, 1, 1)
        dk = dk + mm(ds, qh, 0, 0)
        dvs.append(mm(w16, ng, 0, 0))
    for p in range(H // 2):
        at = slice(2 * p * DV, 2 * (p + 1) * DV)
        out[:, at] = jnp.concatenate(outs[2 * p : 2 * p + 2], 1)
        ggate[:, at] = jnp.concatenate(ggates[2 * p : 2 * p + 2], 1)
        dv_out[:, at] = jnp.concatenate(dvs[2 * p : 2 * p + 2], 1)
    store_state(state_out, states, norms)
    dq_out[...] = dq
    dk_out[...] = dk


def value_kernel(mixed, values, state, dq_in, dk_in, dv_in, first, second, rows, gv, gm):
    keys = mixed[:, H * F :].astype(BF16)
    incoming = state[...]
    norm_rows = incoming[NORM_ROW : NORM_ROW + 16].astype(F32)
    dk = dk_in[...]
    dvs = []
    for h in range(H):
        at = slice(h * FP, (h + 1) * FP)
        first_h, second_h = first[:, at], second[:, at]
        one = mm(keys, first_h) + rows[0:1, at]
        two = mm(keys, second_h) + rows[1:2, at]
        state_h = head_state(incoming, h)
        dphi = mm(head_slice(values, h), state_h) + head_norm(norm_rows, h)
        dk = dk + mm((dphi * two).astype(BF16), first_h, 1, 1)
        dk = dk + mm((dphi * one).astype(BF16), second_h, 1, 1)
        dvs.append(mm((one * two).astype(BF16), state_h, 1, 1))
    for p in range(H // 2):
        at = slice(2 * p * DV, 2 * (p + 1) * DV)
        gv[:, at] = (dv_in[:, at] + jnp.concatenate(dvs[2 * p : 2 * p + 2], 1)).astype(BF16)
    gm[:, : H * F] = dq_in[...]
    gm[:, H * F :] = dk


def hidden_kernel(gm, later, conv, weight, gp_out, gh):
    length = gm.shape[0]
    extended = jnp.concatenate([gm[...], later[...]], 0)
    gp = conv[0:1, :] * extended[0:length]
    for j in range(1, KCONV):
        gp = gp + conv[j : j + 1, :] * extended[j : j + length]
    gp = gp.astype(BF16)
    gp_out[...] = gp
    gh[...] = mm(gp, weight[...], 1, 1).astype(BF16)


def remote(src, dst, s, r, device):
    return pltpu.make_async_remote_copy(
        src_ref=src, dst_ref=dst, send_sem=s, recv_sem=r, device_id=device, device_id_type=MESH
    )


def each(count, f, least=1):
    if count <= least:
        return

    def step(off, c):
        f(off)
        return c

    lax.fori_loop(least, count, step, 0)


def greet(device):
    pl.semaphore_signal(
        pltpu.get_barrier_semaphore(), inc=1, device_id=device, device_id_type=MESH
    )


def scan_kernel(n, backward, *refs):
    if backward:
        state, out, theirs, both, got, sums, give, *sems = refs
        team = 1
    else:
        state, hidden, out, hid, theirs, both, got, sums, give, *sems = refs
        team = 8
        width = hidden.shape[1] // team
        sh, rh = sems[8:]
    s0, r0, s1, r1, s2, r2, s3, r3 = sems[:8]
    dp, me = lax.axis_index("dp"), lax.axis_index("ctx")
    core, pair = lax.rem(me, 2), me // 2
    half = n // 2
    other = (dp, pair * 2 + 1 - core)
    mine = dp * 4 + lax.rem(me, 4)

    def peer(off):
        return lax.rem(pair + off, half)

    def slot(off):
        return lax.rem(pair + half - off, half)

    def far(off):
        return (dp, peer(off) * 2 + core)

    def mate(off):
        return lax.rem(mine + off, team)

    def member(i):
        return (i // 4, me // 4 * 4 + lax.rem(i, 4))

    def columns(i):
        return pl.ds(pl.multiple_of(i * width, width), width)

    def copy0():
        return remote(state.at[1 - core], theirs, s0.at[0], r0.at[0], other)

    def copy1(off):
        return remote(both.at[peer(off)], got.at[pair], s1.at[off], r1.at[off], far(off))

    def copy2(off):
        return remote(sums.at[peer(off)], give.at[0, pair], s2.at[off], r2.at[off], far(off))

    def copy3(off):
        at = slot(off)
        return remote(give.at[1, at], out.at[core, at], s3.at[off], r3.at[off], other)

    def copy_hid(off):
        return remote(
            hidden.at[:, columns(mate(off))], hid.at[mine], sh.at[off], rh.at[off], member(mate(off))
        )

    barrier = pltpu.get_barrier_semaphore()
    greet(other)
    each(half, lambda off: greet(far(off)))
    each(team, lambda off: greet(member(mate(off))))
    pl.semaphore_wait(barrier, half + team - 1)

    copy0().start()
    each(team, lambda off: copy_hid(off).start())
    if team > 1:
        hid[mine] = hidden[:, columns(mine)]
    copy0().wait_recv()
    both[...] = (state[core].astype(F32) + theirs[...].astype(F32)).astype(BF16)
    each(half, lambda off: copy1(off).start())
    got[pair] = both[pair]
    each(half, lambda off: copy1(off).wait_recv())

    def add(i, total):
        at = half - 1 - i if backward else i
        sums[at] = total.astype(BF16)
        return total + got[at].astype(F32)

    lax.fori_loop(0, half, add, jnp.zeros(got.shape[1:], F32))
    each(half, lambda off: copy2(off).start())
    give[0, pair] = sums[pair]
    late = core if not backward else 1 - core
    mine_late = late.astype(F32)
    other_late = 1.0 - mine_late

    def hand_on(off):
        at = slot(off)
        before = give[0, at].astype(F32)
        out[core, at] = (before + mine_late * theirs[at].astype(F32)).astype(BF16)
        give[1, at] = (before + other_late * state[core, at].astype(F32)).astype(BF16)
        copy3(off).start()

    def arrive(off):
        copy2(off).wait_recv()
        hand_on(off)

    hand_on(0)
    each(half, arrive)
    each(half, lambda off: copy3(off).wait_recv(), 0)
    each(half, lambda off: copy3(off).wait_send(), 0)
    each(half, lambda off: copy2(off).wait_send())
    each(half, lambda off: copy1(off).wait_send())
    copy0().wait_send()
    each(team, lambda off: copy_hid(off).wait())


def weight_kernel(n, gp, hid, out, gps, part, got, sa, ra, sb, rb, sc, rc, sd, rd, se, re):
    dp, me = lax.axis_index("dp"), lax.axis_index("ctx")
    count = n // 4
    place, sub = me // 4, lax.rem(me, 4)
    row, core = sub // 2, lax.rem(sub, 2)
    own = dp * 4 + sub

    def peer(off):
        return lax.rem(place + off, count)

    def slot(off):
        return lax.rem(place + count - off, count)

    def far(off):
        return (dp, peer(off) * 4 + sub)

    def side(dx, dy):
        return lax.rem(dp + dx, 2), lax.rem(row + dy, 2) * 2 + core

    def device(dx, dy):
        x, low = side(dx, dy)
        return (x, place * 4 + low)

    def ident(dx, dy):
        x, low = side(dx, dy)
        return x * 4 + low

    other = (dp, place * 4 + row * 2 + 1 - core)
    sides = [(0, 0), (0, 1), (1, 0), (1, 1)]

    def copy_gp(r):
        return remote(gp, gps.at[own], sa.at[r], ra.at[r], device(*sides[r]))

    def copy_gp_on(r):
        ref = gps.at[ident(*sides[r])]
        return remote(gp if r == 0 else ref, ref, sb.at[r], rb.at[r], other)

    def copy_part(off):
        return remote(part.at[peer(off)], got.at[place], sc.at[off], rc.at[off], far(off))

    def copy_sum(off):
        ref = out.at[own, place]
        return remote(ref, ref, sd.at[off], rd.at[off], far(off))

    def copy_on(key, off):
        first, second = ((0, 1), (1, 0)) if off % 2 == 0 else ((1, 0), (0, 1))
        source = ((0, 0), (0, 0), first, (0, 0), first, second, (1, 1))[key]
        target = other if key > 2 else device(*(first if key == 0 else second))
        ref = out.at[ident(*source), slot(off)]
        return remote(ref, ref, se.at[key, off], re.at[key, off], target)

    barrier = pltpu.get_barrier_semaphore()
    greet(other)
    for r in range(1, 4):
        greet(device(*sides[r]))
    each(count, lambda off: greet(far(off)))
    pl.semaphore_wait(barrier, count + 3)

    for r in range(1, 4):
        copy_gp(r).start()
    copy_gp_on(0).start()
    gps[own] = gp[...]
    for r in range(1, 4):
        copy_gp(r).wait_recv()
        copy_gp_on(r).start()
    for r in range(4):
        copy_gp_on(r).wait_recv()
    total = mm(hid[0], gps[0], 0, 0)
    for i in range(1, 8):
        total = total + mm(hid[i], gps[i], 0, 0)
    part[...] = total.reshape(part.shape).astype(BF16)
    each(count, lambda off: copy_part(off).start())
    got[place] = part[place]
    each(count, lambda off: copy_part(off).wait_recv())

    def add(i, total):
        return total + got[i].astype(F32)

    out[own, place] = lax.fori_loop(0, count, add, jnp.zeros(got.shape[1:], F32)).astype(BF16)
    each(count, lambda off: copy_sum(off).start())
    for step in range(count + 2):
        if step < count:
            if step:
                copy_sum(step).wait_recv()
            for key in (1, 0, 3):
                copy_on(key, step).start()
        if 0 <= step - 1 < count:
            copy_on(0, step - 1).wait_recv()
            copy_on(2, step - 1).start()
            copy_on(4, step - 1).start()
            copy_on(1, step - 1).wait_recv()
            copy_on(5, step - 1).start()
        if step >= 2:
            copy_on(2, step - 2).wait_recv()
            copy_on(6, step - 2).start()
    for off in range(count):
        for key in range(7):
            if key > 2:
                copy_on(key, off).wait_recv()
            copy_on(key, off).wait_send()
    each(count, lambda off: copy_sum(off).wait_send())
    each(count, lambda off: copy_part(off).wait_send())
    for r in range(4):
        if r:
            copy_gp(r).wait_send()
        copy_gp_on(r).wait_send()


def call(kernel, ins, outs, scratch=(), collective=None):
    extra = {} if collective is None else dict(collective_id=collective, has_side_effects=True)
    return pl.pallas_call(
        kernel,
        out_shape=[jax.ShapeDtypeStruct(s, t) for s, t in outs],
        in_specs=[VM] * len(ins),
        out_specs=[VM] * len(outs),
        scratch_shapes=list(scratch),
        compiler_params=pltpu.CompilerParams(vmem_limit_bytes=48 * 2**20, **extra),
    )(*ins)


def scan(state, n, hidden=None):
    half = n // 2
    halves = state.reshape(2, half, -1, 128)
    ins, outs = [halves], [(halves.shape, BF16)]
    sem = pltpu.SemaphoreType.DMA
    sems = [sem((1,))] * 2 + [sem((half,))] * 6
    if hidden is not None:
        ins.append(hidden)
        outs.append(((8, hidden.shape[0], hidden.shape[1] // 8), BF16))
        sems = sems + [sem((8,))] * 2
    scratch = [pltpu.VMEM(halves.shape[1:], BF16)] * 4 + [pltpu.VMEM(halves.shape, BF16)]
    out, *rest = call(
        functools.partial(scan_kernel, n, hidden is None), ins, outs, scratch + sems,
        collective=1 if hidden is None else 0,
    )
    return out.reshape(-1, 128), *rest


def shifted(array, axis, by):
    length = lax.axis_size(axis)
    pairs = [(i, i + by) for i in range(length) if 0 <= i + by < length]
    return lax.ppermute(array, axis, pairs)


def body(n, hidden_in, qk_weight, conv_weight, values, gate_in, cotangent):
    tokens, v, gate, cot = hidden_in[0], values[0], gate_in[0], cotangent[0]
    length, depth = tokens.shape
    cols = qk_weight.shape[1]
    wide = v.shape[1]
    first, second, rows = feature_tables()
    tables = [jnp.asarray(first, BF16), jnp.asarray(second, BF16), jnp.asarray(rows)]
    state_rows = n * 16 * -(-(NORM_ROW + 16) // (16 * n))
    state_shape = ((state_rows, 128), BF16)

    projected = jnp.dot(tokens, qk_weight, preferred_element_type=F32).astype(BF16)
    prev = shifted(projected[length - 8 :], "ctx", 1).astype(F32)
    mixed, own = call(
        key_kernel, [projected, prev, conv_weight, v, *tables], [((length, cols), F32), state_shape]
    )
    before, hid = scan(own, n, tokens)
    out, ggate, own_grad, dq, dk, dv = call(
        query_kernel,
        [mixed, v, gate, cot, before, *tables],
        [
            ((length, wide), BF16), ((length, wide), BF16), state_shape,
            ((length, cols // 2), F32), ((length, cols // 2), F32), ((length, wide), F32),
        ],
    )
    (after,) = scan(own_grad, n)
    gv, gm = call(
        value_kernel, [mixed, v, after, dq, dk, dv, *tables],
        [((length, wide), BF16), ((length, cols), F32)],
    )
    later = shifted(gm[:8], "ctx", -1)
    gp, gh = call(
        hidden_kernel, [gm, later, conv_weight, qk_weight],
        [((length, cols), BF16), ((length, depth), BF16)],
    )
    count = n // 4
    piece = depth // (8 * count)
    sem = pltpu.SemaphoreType.DMA
    (gw,) = call(
        functools.partial(weight_kernel, n), [gp, hid], [((8, count, piece, cols), BF16)],
        [
            pltpu.VMEM((8, length, cols), BF16),
            pltpu.VMEM((count, piece, cols), BF16),
            pltpu.VMEM((count, piece, cols), BF16),
        ]
        + [sem((4,))] * 4 + [sem((count,))] * 4 + [sem((7, count))] * 2,
        collective=2,
    )
    return out[None], gh[None], gv[None], ggate[None], gw.reshape(depth, cols)


def solution(mesh):
    split = P("dp", "ctx", None)
    return jax.shard_map(
        functools.partial(body, mesh.shape["ctx"]),
        mesh=mesh,
        in_specs=(split, P(), P(), split, split, split),
        out_specs=(split, split, split, split, P()),
        check_vma=False,
    )
```

```python
import functools

import jax
import jax.numpy as jnp
import numpy as np
from jax import lax
from jax.experimental import pallas as pl
from jax.experimental.pallas import tpu as pltpu
from jax.sharding import PartitionSpec as P

H = 8
F = 16
DV = 64
KCONV = 3
FP = 256
F32 = jnp.float32
BF16 = jnp.bfloat16
MESH = pl.DeviceIdType.MESH
VM = pl.BlockSpec(memory_space=pltpu.VMEM)
NORM_ROW = H * DV + 2 * DV


def feature_tables():
    pairs = [(a, b) for a in range(F + 1) for b in range(a, F + 1)]
    first = np.zeros((H * F, H * FP), np.float32)
    second = np.zeros((H * F, H * FP), np.float32)
    rows = np.zeros((8, H * FP), np.float32)
    for h in range(H):
        for m, (a, b) in enumerate(pairs):
            lane = h * FP + (m if m < 128 else 128 + 32 * (h % 4) + m - 128)
            if a:
                first[h * F + a - 1, lane] = 1.0
            else:
                rows[0, lane] = 1.0
            if b:
                second[h * F + b - 1, lane] = 1.0
            else:
                rows[1, lane] = 1.0
            scale = 1.0 if b == 0 else 1.0 / F**0.5 if a == 0 else 1.0 / F
            rows[2, lane] = scale * (0.5 if a == b and a else 1.0)
    return first, second, rows


def mm(a, b, ca=1, cb=0):
    return lax.dot_general(a, b, (((ca,), (cb,)), ((), ())), preferred_element_type=F32)


def head_slice(array, h):
    return array[:, h * DV : (h + 1) * DV]


def head_state(state, h):
    tail = H * DV + (h // 4) * DV
    return jnp.concatenate(
        [state[h * DV : (h + 1) * DV], state[tail : tail + DV]], 1
    )


def head_norm(norms, h):
    tail = H + h // 4
    return jnp.concatenate([norms[h : h + 1], norms[tail : tail + 1]], 1)


def store_state(ref, states, norms):
    for h in range(H):
        ref[h * DV : (h + 1) * DV, :] = states[h][:, :128].astype(BF16)
    for g in range(2):
        tail = sum(states[4 * g + i][:, 128:] for i in range(4))
        ref[H * DV + g * DV : H * DV + (g + 1) * DV, :] = tail.astype(BF16)
    rows = [norms[h][:, :128] for h in range(H)]
    rows += [sum(norms[4 * g + i][:, 128:] for i in range(4)) for g in range(2)]
    rows.append(jnp.zeros((16 - len(rows), 128), F32))
    ref[NORM_ROW : NORM_ROW + 16, :] = jnp.concatenate(rows, 0).astype(BF16)
    rest = ref.shape[0] - NORM_ROW - 16
    if rest:
        ref[NORM_ROW + 16 :, :] = jnp.zeros((rest, 128), BF16)


def mix(proj, prev, conv, mixed_out):
    length = proj.shape[0]
    padded = jnp.concatenate([prev[8:, :].astype(F32), proj[...].astype(F32)], 0)
    mixed = conv[0:1, :] * padded[8 : 8 + length]
    for j in range(1, KCONV):
        mixed = mixed + conv[j : j + 1, :] * padded[8 - j : 8 - j + length]
    mixed_out[...] = mixed


def key_part(mixed, values, first, second, rows, state_out):
    keys = mixed[:, H * F :].astype(BF16)
    states, norms = [], []
    for h in range(H):
        at = slice(h * FP, (h + 1) * FP)
        phi = (mm(keys, first[:, at]) + rows[0:1, at]) * (mm(keys, second[:, at]) + rows[1:2, at])
        states.append(mm(head_slice(values, h), phi.astype(BF16), 0, 0))
        norms.append(jnp.sum(phi, 0, keepdims=True))
    store_state(state_out, states, norms)


def query_part(
    mixed, values, gate, cot, state, first, second, rows, out, ggate, state_out, dq_out, dk_out, dv_out
):
    length = mixed.shape[0]
    q = mixed[:, : H * F].astype(BF16)
    k = mixed[:, H * F :].astype(BF16)
    lane = lax.broadcasted_iota(jnp.int32, (length, H * F), 1) // F
    causal = lax.broadcasted_iota(jnp.int32, (length, length), 0) >= lax.broadcasted_iota(
        jnp.int32, (length, length), 1
    )
    zero = jnp.zeros_like(q)
    incoming = state[...]
    norm_rows = incoming[NORM_ROW : NORM_ROW + 16].astype(F32)
    dq = jnp.zeros((length, H * F), F32)
    dk = jnp.zeros((length, H * F), F32)
    states, norms, outs, ggates, dvs = [], [], [], [], []
    for h in range(H):
        at = slice(h * FP, (h + 1) * FP)
        first_h, second_h, scale = first[:, at], second[:, at], rows[2:3, at]
        qh = jnp.where(lane == h, q, zero)
        kh = jnp.where(lane == h, k, zero)
        v = head_slice(values, h)
        s = mm(qh, k, 1, 1) * F**-0.5
        w = jnp.where(causal, 1.0 + s + 0.5 * s * s, 0.0)
        w16 = w.astype(BF16)
        one = mm(q, first_h) + rows[0:1, at]
        two = (mm(q, second_h) + rows[1:2, at]) * scale
        phi = one * two
        phi16 = phi.astype(BF16)
        state_h = head_state(incoming, h)
        norm_h = head_norm(norm_rows, h)
        den = jnp.sum(w, 1, keepdims=True) + jnp.sum(phi * norm_h, 1, keepdims=True)
        inv = 1.0 / den
        att = (mm(w16, v) + mm(phi16, state_h, 1, 1)) * inv
        g = head_slice(gate, h).astype(F32)
        up = head_slice(cot, h).astype(F32)
        sig = 1.0 / (1.0 + jnp.exp(-g))
        act = g * sig
        ga = up * act
        gd = -jnp.sum(ga * att, 1, keepdims=True) * inv
        ng = (ga * inv).astype(BF16)
        outs.append((att * act).astype(BF16))
        ggates.append((up * att * sig * (1.0 + g * (1.0 - sig))).astype(BF16))
        states.append(mm(ng, phi16, 0, 0))
        norms.append(jnp.sum(gd * phi, 0, keepdims=True))
        dw = mm(ng, v, 1, 1) + gd
        ds = (jnp.where(causal, dw * (1.0 + s), 0.0) * F**-0.5).astype(BF16)
        dphi = mm(ng, state_h) + gd * norm_h
        dq = dq + mm(ds, kh)
        dq = dq + mm((dphi * two).astype(BF16), first_h, 1, 1)
        dq = dq + mm((dphi * one * scale).astype(BF16), second_h, 1, 1)
        dk = dk + mm(ds, qh, 0, 0)
        dvs.append(mm(w16, ng, 0, 0))
    for p in range(H // 2):
        at = slice(2 * p * DV, 2 * (p + 1) * DV)
        out[:, at] = jnp.concatenate(outs[2 * p : 2 * p + 2], 1)
        ggate[:, at] = jnp.concatenate(ggates[2 * p : 2 * p + 2], 1)
        dv_out[:, at] = jnp.concatenate(dvs[2 * p : 2 * p + 2], 1)
    store_state(state_out, states, norms)
    dq_out[...] = dq
    dk_out[...] = dk


def value_part(mixed, values, state, dq_in, dk_in, dv_in, first, second, rows, gv, gm):
    keys = mixed[:, H * F :].astype(BF16)
    incoming = state[...]
    norm_rows = incoming[NORM_ROW : NORM_ROW + 16].astype(F32)
    dk = dk_in[...]
    dvs = []
    for h in range(H):
        at = slice(h * FP, (h + 1) * FP)
        first_h, second_h = first[:, at], second[:, at]
        one = mm(keys, first_h) + rows[0:1, at]
        two = mm(keys, second_h) + rows[1:2, at]
        state_h = head_state(incoming, h)
        dphi = mm(head_slice(values, h), state_h) + head_norm(norm_rows, h)
        dk = dk + mm((dphi * two).astype(BF16), first_h, 1, 1)
        dk = dk + mm((dphi * one).astype(BF16), second_h, 1, 1)
        dvs.append(mm((one * two).astype(BF16), state_h, 1, 1))
    for p in range(H // 2):
        at = slice(2 * p * DV, 2 * (p + 1) * DV)
        gv[:, at] = (dv_in[:, at] + jnp.concatenate(dvs[2 * p : 2 * p + 2], 1)).astype(BF16)
    gm[:, : H * F] = dq_in[...]
    gm[:, H * F :] = dk


def project_back(gm, later, conv, gp_out):
    length = gm.shape[0]
    extended = jnp.concatenate([gm[...], later[...]], 0)
    gp = conv[0:1, :] * extended[0:length]
    for j in range(1, KCONV):
        gp = gp + conv[j : j + 1, :] * extended[j : j + length]
    gp_out[...] = gp.astype(BF16)


def remote(src, dst, s, r, device):
    return pltpu.make_async_remote_copy(
        src_ref=src, dst_ref=dst, send_sem=s, recv_sem=r, device_id=device, device_id_type=MESH
    )


def each(count, f, least=1):
    if count <= least:
        return

    def step(off, c):
        f(off)
        return c

    lax.fori_loop(least, count, step, 0)


def greet(device):
    pl.semaphore_signal(
        pltpu.get_barrier_semaphore(), inc=1, device_id=device, device_id_type=MESH
    )


def scan_part(n, backward, state, out, theirs, both, got, sums, give, s0, r0, s1, r1, s2, r2, s3, r3):
    dp, me = lax.axis_index("dp"), lax.axis_index("ctx")
    core, pair = lax.rem(me, 2), me // 2
    half = n // 2
    size = got.shape[1]
    other = (dp, pair * 2 + 1 - core)

    def peer(off):
        return lax.rem(pair + off, half)

    def slot(off):
        return lax.rem(pair + half - off, half)

    def far(off):
        return (dp, peer(off) * 2 + core)

    def part(at, count=1):
        return pl.ds(pl.multiple_of(at * size, 16), count * size)

    def copy0():
        return remote(state.at[part((1 - core) * half, half)], theirs, s0.at[0], r0.at[0], other)

    def copy1(off):
        return remote(both.at[part(peer(off))], got.at[pair], s1.at[off], r1.at[off], far(off))

    def copy2(off):
        return remote(sums.at[peer(off)], give.at[0, pair], s2.at[off], r2.at[off], far(off))

    def copy3(off):
        at = slot(off)
        return remote(
            give.at[1, at], out.at[part(core * half + at)], s3.at[off], r3.at[off], other
        )

    copy0().start()
    copy0().wait_recv()
    both[...] = (state[part(core * half, half)].astype(F32) + theirs[...].astype(F32)).astype(BF16)
    each(half, lambda off: copy1(off).start())
    got[pair] = both[part(pair)]
    each(half, lambda off: copy1(off).wait_recv())

    def add(i, total):
        at = half - 1 - i if backward else i
        sums[at] = total.astype(BF16)
        return total + got[at].astype(F32)

    lax.fori_loop(0, half, add, jnp.zeros(got.shape[1:], F32))
    each(half, lambda off: copy2(off).start())
    give[0, pair] = sums[pair]
    late = core if not backward else 1 - core
    mine_late = late.astype(F32)
    other_late = 1.0 - mine_late

    def hand_on(off):
        at = slot(off)
        before = give[0, at].astype(F32)
        own = part(core * half + at)
        give[1, at] = (before + other_late * state[own].astype(F32)).astype(BF16)
        copy3(off).start()
        out[own] = (before + mine_late * theirs[part(at)].astype(F32)).astype(BF16)

    def arrive(off):
        copy2(off).wait_recv()
        hand_on(off)

    hand_on(0)
    each(half, arrive)
    each(half, lambda off: copy3(off).wait_recv(), 0)

    def finish():
        each(half, lambda off: copy3(off).wait_send(), 0)
        each(half, lambda off: copy2(off).wait_send())
        each(half, lambda off: copy1(off).wait_send())
        copy0().wait_send()

    return finish


def layer_kernel(n, *refs):
    hidden, weight, conv, values, gate, cot, first, second, rows = refs[:9]
    out, gh, gv, ggate, gw = refs[9:14]
    proj, prev, later, mixed, state, before, grad_state, after = refs[14:22]
    dq, dk, dv, gm, gp, hid, gps, part, got = refs[22:31]
    scan1, scan2 = refs[31:36], refs[36:41]
    sems1, sems2 = refs[41:49], refs[49:57]
    sh, rh, halo, sa, ra, sb, rb, sc, rc, sd, rd, se, re = refs[57:]
    tables = (first, second, rows)
    length = hidden.shape[0]

    dp, me = lax.axis_index("dp"), lax.axis_index("ctx")
    count = n // 4
    place, sub = me // 4, lax.rem(me, 4)
    row, core = sub // 2, lax.rem(sub, 2)
    own = dp * 4 + sub
    width = hid.shape[2]

    def peer(off):
        return lax.rem(place + off, count)

    def slot(off):
        return lax.rem(place + count - off, count)

    def far(off):
        return (dp, peer(off) * 4 + sub)

    def side(dx, dy):
        return lax.rem(dp + dx, 2), lax.rem(row + dy, 2) * 2 + core

    def device(dx, dy):
        x, low = side(dx, dy)
        return (x, place * 4 + low)

    def ident(dx, dy):
        x, low = side(dx, dy)
        return x * 4 + low

    other = (dp, place * 4 + row * 2 + 1 - core)
    sides = [(0, 0), (0, 1), (1, 0), (1, 1)]

    def mate(off):
        return lax.rem(own + off, 8)

    def member(i):
        return (i // 4, place * 4 + lax.rem(i, 4))

    def columns(i):
        return pl.ds(pl.multiple_of(i * width, width), width)

    def copy_hid(off):
        return remote(
            hidden.at[:, columns(mate(off))], hid.at[own], sh.at[off], rh.at[off], member(mate(off))
        )

    def copy_prev():
        return remote(proj.at[pl.ds(length - 16, 16)], prev, halo.at[0], halo.at[1], (dp, me + 1))

    def copy_later():
        return remote(gm.at[pl.ds(0, 8)], later, halo.at[2], halo.at[3], (dp, me - 1))

    def copy_gp(r):
        return remote(gp, gps.at[own], sa.at[r], ra.at[r], device(*sides[r]))

    def copy_gp_on(r):
        ref = gps.at[ident(*sides[r])]
        return remote(gp if r == 0 else ref, ref, sb.at[r], rb.at[r], other)

    def copy_part(off):
        return remote(part.at[peer(off)], got.at[place], sc.at[off], rc.at[off], far(off))

    def copy_sum(off):
        ref = gw.at[own, place]
        return remote(ref, ref, sd.at[off], rd.at[off], far(off))

    def copy_on(key, off):
        one, two = ((0, 1), (1, 0)) if off % 2 == 0 else ((1, 0), (0, 1))
        source = ((0, 0), (0, 0), one, (0, 0), one, two, (1, 1))[key]
        target = other if key > 2 else device(*(one if key == 0 else two))
        ref = gw.at[ident(*source), slot(off)]
        return remote(ref, ref, se.at[key, off], re.at[key, off], target)

    barrier = pltpu.get_barrier_semaphore()
    each(n, lambda off: greet((dp, lax.rem(me + off, n))))
    each(4, lambda i: greet((1 - dp, place * 4 + i)), 0)
    proj[...] = mm(hidden[...], weight[...]).astype(BF16)
    pl.semaphore_wait(barrier, n + 3)

    @pl.when(me < n - 1)
    def _():
        copy_prev().start()

    each(8, lambda off: copy_hid(off).start())
    hid[own] = hidden[:, columns(own)]

    @pl.when(me > 0)
    def _():
        copy_prev().wait_recv()

    @pl.when(me == 0)
    def _():
        prev[...] = jnp.zeros(prev.shape, BF16)

    mix(proj, prev, conv, mixed)
    key_part(mixed, values, *tables, state)
    finish1 = scan_part(n, False, state, before, *scan1, *sems1)
    query_part(mixed, values, gate, cot, before, *tables, out, ggate, grad_state, dq, dk, dv)
    finish2 = scan_part(n, True, grad_state, after, *scan2, *sems2)
    value_part(mixed, values, after, dq, dk, dv, *tables, gv, gm)

    @pl.when(me > 0)
    def _():
        copy_later().start()

    @pl.when(me < n - 1)
    def _():
        copy_later().wait_recv()

    @pl.when(me == n - 1)
    def _():
        later[...] = jnp.zeros(later.shape, F32)

    project_back(gm, later, conv, gp)
    for r in range(1, 4):
        copy_gp(r).start()
    copy_gp_on(0).start()
    gps[own] = gp[...]
    gh[...] = mm(gp[...], weight[...], 1, 1).astype(BF16)
    each(8, lambda off: copy_hid(off).wait_recv())
    for r in range(1, 4):
        copy_gp(r).wait_recv()
        copy_gp_on(r).start()
    for r in range(4):
        copy_gp_on(r).wait_recv()
    total = mm(hid[0], gps[0], 0, 0)
    for i in range(1, 8):
        total = total + mm(hid[i], gps[i], 0, 0)
    part[...] = total.reshape(part.shape).astype(BF16)
    each(count, lambda off: copy_part(off).start())
    got[place] = part[place]
    each(count, lambda off: copy_part(off).wait_recv())

    def add(i, total):
        return total + got[i].astype(F32)

    gw[own, place] = lax.fori_loop(0, count, add, jnp.zeros(got.shape[1:], F32)).astype(BF16)
    each(count, lambda off: copy_sum(off).start())
    for step in range(count + 2):
        if step < count:
            if step:
                copy_sum(step).wait_recv()
            for key in (1, 0, 3):
                copy_on(key, step).start()
        if 0 <= step - 1 < count:
            copy_on(0, step - 1).wait_recv()
            copy_on(2, step - 1).start()
            copy_on(4, step - 1).start()
            copy_on(1, step - 1).wait_recv()
            copy_on(5, step - 1).start()
        if step >= 2:
            copy_on(2, step - 2).wait_recv()
            copy_on(6, step - 2).start()
    for off in range(count):
        for key in range(7):
            if key > 2:
                copy_on(key, off).wait_recv()
            copy_on(key, off).wait_send()
    each(count, lambda off: copy_sum(off).wait_send())
    each(count, lambda off: copy_part(off).wait_send())
    for r in range(4):
        if r:
            copy_gp(r).wait_send()
        copy_gp_on(r).wait_send()
    finish1()
    finish2()
    each(8, lambda off: copy_hid(off).wait_send())

    @pl.when(me < n - 1)
    def _():
        copy_prev().wait_send()

    @pl.when(me > 0)
    def _():
        copy_later().wait_send()


def body(n, hidden_in, qk_weight, conv_weight, values, gate_in, cotangent):
    tokens, v, gate, cot = hidden_in[0], values[0], gate_in[0], cotangent[0]
    length, depth = tokens.shape
    cols = qk_weight.shape[1]
    wide = v.shape[1]
    first, second, rows = feature_tables()
    half, count = n // 2, n // 4
    size = 16 * -(-(NORM_ROW + 16) // (16 * n))
    piece = depth // (8 * count)
    sem, vmem = pltpu.SemaphoreType.DMA, pltpu.VMEM
    state = vmem((n * size, 128), BF16)
    scan = [
        vmem((half * size, 128), BF16), vmem((half * size, 128), BF16),
        vmem((half, size, 128), BF16), vmem((half, size, 128), BF16),
        vmem((2, half, size, 128), BF16),
    ]
    scan_sems = [sem((1,))] * 2 + [sem((half,))] * 6
    outs = [
        ((length, wide), BF16), ((length, depth), BF16), ((length, wide), BF16),
        ((length, wide), BF16), ((8, count, piece, cols), BF16),
    ]
    out, gh, gv, ggate, gw = pl.pallas_call(
        functools.partial(layer_kernel, n),
        out_shape=[jax.ShapeDtypeStruct(s, t) for s, t in outs],
        in_specs=[VM] * 9,
        out_specs=[VM] * 5,
        scratch_shapes=[
            vmem((length, cols), BF16), vmem((16, cols), BF16), vmem((8, cols), F32),
            vmem((length, cols), F32), state, state, state, state,
            vmem((length, cols // 2), F32), vmem((length, cols // 2), F32),
            vmem((length, wide), F32), vmem((length, cols), F32), vmem((length, cols), BF16),
            vmem((8, length, depth // 8), BF16), vmem((8, length, cols), BF16),
            vmem((count, piece, cols), BF16), vmem((count, piece, cols), BF16),
        ]
        + scan * 2 + scan_sems * 2
        + [sem((8,))] * 2 + [sem((4,))] * 5 + [sem((count,))] * 4 + [sem((7, count))] * 2,
        compiler_params=pltpu.CompilerParams(
            vmem_limit_bytes=48 * 2**20, collective_id=0, has_side_effects=True
        ),
    )(
        tokens, qk_weight, conv_weight, v, gate, cot,
        jnp.asarray(first, BF16), jnp.asarray(second, BF16), jnp.asarray(rows),
    )
    return out[None], gh[None], gv[None], ggate[None], gw.reshape(depth, cols)


def solution(mesh):
    split = P("dp", "ctx", None)
    return jax.shard_map(
        functools.partial(body, mesh.shape["ctx"]),
        mesh=mesh,
        in_specs=(split, P(), P(), split, split, split),
        out_specs=(split, split, split, split, P()),
        check_vma=False,
    )
```

```python
import functools

import jax
import jax.numpy as jnp
import numpy as np
from jax import lax
from jax.experimental import pallas as pl
from jax.experimental.pallas import tpu as pltpu
from jax.sharding import PartitionSpec as P

H = 8
F = 16
DV = 64
KCONV = 3
FP = 256
F32 = jnp.float32
BF16 = jnp.bfloat16
MESH = pl.DeviceIdType.MESH
VM = pl.BlockSpec(memory_space=pltpu.VMEM)
NORM_ROW = H * DV + 2 * DV


def feature_tables():
    pairs = [(a, b) for a in range(F + 1) for b in range(a, F + 1)]
    first = np.zeros((H * F, H * FP), np.float32)
    second = np.zeros((H * F, H * FP), np.float32)
    rows = np.zeros((8, H * FP), np.float32)
    for h in range(H):
        for m, (a, b) in enumerate(pairs):
            lane = h * FP + (m if m < 128 else 128 + 32 * (h % 4) + m - 128)
            if a:
                first[h * F + a - 1, lane] = 1.0
            else:
                rows[0, lane] = 1.0
            if b:
                second[h * F + b - 1, lane] = 1.0
            else:
                rows[1, lane] = 1.0
            scale = 1.0 if b == 0 else 1.0 / F**0.5 if a == 0 else 1.0 / F
            rows[2, lane] = scale * (0.5 if a == b and a else 1.0)
    return first, second, rows


def mm(a, b, ca=1, cb=0):
    return lax.dot_general(a, b, (((ca,), (cb,)), ((), ())), preferred_element_type=F32)


def head_slice(array, h):
    return array[:, h * DV : (h + 1) * DV]


def head_state(state, h):
    tail = H * DV + (h // 4) * DV
    return jnp.concatenate(
        [state[h * DV : (h + 1) * DV], state[tail : tail + DV]], 1
    )


def head_norm(norms, h):
    tail = H + h // 4
    return jnp.concatenate([norms[h : h + 1], norms[tail : tail + 1]], 1)


def store_state(ref, states):
    for h in range(H):
        ref[h * DV : (h + 1) * DV, :] = states[h][:, :128].astype(BF16)
    for g in range(2):
        tail = sum(states[4 * g + i][:, 128:] for i in range(4))
        ref[H * DV + g * DV : H * DV + (g + 1) * DV, :] = tail.astype(BF16)
    rest = ref.shape[0] - NORM_ROW
    if rest:
        ref[NORM_ROW:, :] = jnp.zeros((rest, 128), BF16)


def norm_block(norms):
    rows = [norms[h][:, :128] for h in range(H)]
    rows += [sum(norms[4 * g + i][:, 128:] for i in range(4)) for g in range(2)]
    rows.append(jnp.zeros((16 - len(rows), 128), F32))
    return jnp.concatenate(rows, 0)


def mix(proj, prev, conv, mixed_out):
    length = proj.shape[0]
    padded = jnp.concatenate([prev[8:, :].astype(F32), proj[...].astype(F32)], 0)
    mixed = conv[0:1, :] * padded[8 : 8 + length]
    for j in range(1, KCONV):
        mixed = mixed + conv[j : j + 1, :] * padded[8 - j : 8 - j + length]
    mixed_out[...] = mixed


def key_part(mixed, values, first, second, rows, state_out):
    keys = mixed[:, H * F :].astype(BF16)
    states, norms = [], []
    for h in range(H):
        at = slice(h * FP, (h + 1) * FP)
        phi = (mm(keys, first[:, at]) + rows[0:1, at]) * (mm(keys, second[:, at]) + rows[1:2, at])
        states.append(mm(head_slice(values, h), phi.astype(BF16), 0, 0))
        norms.append(jnp.sum(phi, 0, keepdims=True))
    store_state(state_out, states)
    return norm_block(norms)


def heads_of(mixed):
    lane = lax.broadcasted_iota(jnp.int32, (mixed.shape[0], H * F), 1) // F
    q = mixed[:, : H * F].astype(BF16)
    k = mixed[:, H * F :].astype(BF16)
    zero = jnp.zeros_like(q)
    return q, k, lambda a, h: jnp.where(lane == h, a, zero)


def causal_of(length):
    return lax.broadcasted_iota(jnp.int32, (length, length), 0) >= lax.broadcasted_iota(
        jnp.int32, (length, length), 1
    )


def weights_of(s, causal):
    return jnp.where(causal, 1.0 + s + 0.5 * s * s, 0.0)


def local_part(mixed, values, first, second, rows, s_ref, num_ref, one_ref, two_ref):
    q, k, only = heads_of(mixed)
    causal = causal_of(mixed.shape[0])
    for h in range(H):
        at = slice(h * FP, (h + 1) * FP)
        s = mm(only(q, h), k, 1, 1) * F**-0.5
        s_ref[h] = s
        num_ref[h] = mm(weights_of(s, causal).astype(BF16), head_slice(values, h))
        one_ref[:, at] = mm(q, first[:, at]) + rows[0:1, at]
        two_ref[:, at] = (mm(q, second[:, at]) + rows[1:2, at]) * rows[2:3, at]


def denom_part(norm_rows, gate, cot, s_ref, one_ref, two_ref, ng_ref, inv_ref, state_out):
    causal = causal_of(s_ref.shape[1])
    states = []
    for h in range(H):
        at = slice(h * FP, (h + 1) * FP)
        phi = one_ref[:, at] * two_ref[:, at]
        den = jnp.sum(weights_of(s_ref[h], causal), 1, keepdims=True) + jnp.sum(
            phi * head_norm(norm_rows, h), 1, keepdims=True
        )
        inv = 1.0 / den
        g = head_slice(gate, h).astype(F32)
        ga = head_slice(cot, h).astype(F32) * g / (1.0 + jnp.exp(-g))
        ng = (ga * inv).astype(BF16)
        inv_ref[h] = inv
        ng_ref[h] = ng
        states.append(mm(ng, phi.astype(BF16), 0, 0))
    store_state(state_out, states)


def attend_part(gate, cot, state, num_ref, one_ref, two_ref, inv_ref, gd_ref, out, ggate):
    incoming = state[...]
    norms, outs, ggates = [], [], []
    for h in range(H):
        at = slice(h * FP, (h + 1) * FP)
        phi = one_ref[:, at] * two_ref[:, at]
        inv = inv_ref[h]
        att = (num_ref[h] + mm(phi.astype(BF16), head_state(incoming, h), 1, 1)) * inv
        g = head_slice(gate, h).astype(F32)
        up = head_slice(cot, h).astype(F32)
        sig = 1.0 / (1.0 + jnp.exp(-g))
        act = g * sig
        gd = -jnp.sum(up * act * att, 1, keepdims=True) * inv
        gd_ref[h] = gd
        outs.append((att * act).astype(BF16))
        ggates.append((up * att * sig * (1.0 + g * (1.0 - sig))).astype(BF16))
        norms.append(jnp.sum(gd * phi, 0, keepdims=True))
    for p in range(H // 2):
        at = slice(2 * p * DV, 2 * (p + 1) * DV)
        out[:, at] = jnp.concatenate(outs[2 * p : 2 * p + 2], 1)
        ggate[:, at] = jnp.concatenate(ggates[2 * p : 2 * p + 2], 1)
    return norm_block(norms)


def query_part(
    mixed, values, state, norm_rows, first, second, rows, s_ref, one_ref, two_ref, ng_ref, gd_ref,
    dq_out, dk_out, dv_out,
):
    q, k, only = heads_of(mixed)
    length = mixed.shape[0]
    causal = causal_of(length)
    incoming = state[...]
    dq = jnp.zeros((length, H * F), F32)
    dk = jnp.zeros((length, H * F), F32)
    dvs = []
    for h in range(H):
        at = slice(h * FP, (h + 1) * FP)
        s, ng, gd = s_ref[h], ng_ref[h], gd_ref[h]
        one, two = one_ref[:, at], two_ref[:, at]
        dw = mm(ng, head_slice(values, h), 1, 1) + gd
        ds = (jnp.where(causal, dw * (1.0 + s), 0.0) * F**-0.5).astype(BF16)
        dphi = mm(ng, head_state(incoming, h)) + gd * head_norm(norm_rows, h)
        dq = dq + mm(ds, only(k, h))
        dq = dq + mm((dphi * two).astype(BF16), first[:, at], 1, 1)
        dq = dq + mm((dphi * one * rows[2:3, at]).astype(BF16), second[:, at], 1, 1)
        dk = dk + mm(ds, only(q, h), 0, 0)
        dvs.append(mm(weights_of(s, causal).astype(BF16), ng, 0, 0))
    for p in range(H // 2):
        at = slice(2 * p * DV, 2 * (p + 1) * DV)
        dv_out[:, at] = jnp.concatenate(dvs[2 * p : 2 * p + 2], 1)
    dq_out[...] = dq
    dk_out[...] = dk


def value_part(mixed, values, state, norm_rows, dq_in, dk_in, dv_in, first, second, rows, gv, gm):
    keys = mixed[:, H * F :].astype(BF16)
    incoming = state[...]
    dk = dk_in[...]
    dvs = []
    for h in range(H):
        at = slice(h * FP, (h + 1) * FP)
        first_h, second_h = first[:, at], second[:, at]
        one = mm(keys, first_h) + rows[0:1, at]
        two = mm(keys, second_h) + rows[1:2, at]
        state_h = head_state(incoming, h)
        dphi = mm(head_slice(values, h), state_h) + head_norm(norm_rows, h)
        dk = dk + mm((dphi * two).astype(BF16), first_h, 1, 1)
        dk = dk + mm((dphi * one).astype(BF16), second_h, 1, 1)
        dvs.append(mm((one * two).astype(BF16), state_h, 1, 1))
    for p in range(H // 2):
        at = slice(2 * p * DV, 2 * (p + 1) * DV)
        gv[:, at] = (dv_in[:, at] + jnp.concatenate(dvs[2 * p : 2 * p + 2], 1)).astype(BF16)
    gm[:, : H * F] = dq_in[...]
    gm[:, H * F :] = dk


def project_back(gm, later, conv, gp_out):
    length = gm.shape[0]
    extended = jnp.concatenate([gm[...], later[...]], 0)
    gp = conv[0:1, :] * extended[0:length]
    for j in range(1, KCONV):
        gp = gp + conv[j : j + 1, :] * extended[j : j + length]
    gp_out[...] = gp.astype(BF16)


def remote(src, dst, s, r, device):
    return pltpu.make_async_remote_copy(
        src_ref=src, dst_ref=dst, send_sem=s, recv_sem=r, device_id=device, device_id_type=MESH
    )


def each(count, f, least=1):
    if count <= least:
        return

    def step(off, c):
        f(off)
        return c

    lax.fori_loop(least, count, step, 0)


def greet(device):
    pl.semaphore_signal(
        pltpu.get_barrier_semaphore(), inc=1, device_id=device, device_id_type=MESH
    )


def scan_part(n, backward, state, out, theirs, both, got, sums, give, s0, r0, s1, r1, s2, r2, s3, r3):
    dp, me = lax.axis_index("dp"), lax.axis_index("ctx")
    core, pair = lax.rem(me, 2), me // 2
    half = n // 2
    size = got.shape[1]
    other = (dp, pair * 2 + 1 - core)

    def peer(off):
        return lax.rem(pair + off, half)

    def slot(off):
        return lax.rem(pair + half - off, half)

    def far(off):
        return (dp, peer(off) * 2 + core)

    def part(at, count=1):
        return pl.ds(pl.multiple_of(at * size, 16), count * size)

    def copy0():
        return remote(state.at[part((1 - core) * half, half)], theirs, s0.at[0], r0.at[0], other)

    def copy1(off):
        return remote(both.at[part(peer(off))], got.at[pair], s1.at[off], r1.at[off], far(off))

    def copy2(off):
        return remote(sums.at[peer(off)], give.at[0, pair], s2.at[off], r2.at[off], far(off))

    def copy3(off):
        at = slot(off)
        return remote(
            give.at[1, at], out.at[part(core * half + at)], s3.at[off], r3.at[off], other
        )

    copy0().start()
    yield
    copy0().wait_recv()
    both[...] = (state[part(core * half, half)].astype(F32) + theirs[...].astype(F32)).astype(BF16)
    each(half, lambda off: copy1(off).start())
    got[pair] = both[part(pair)]
    yield
    each(half, lambda off: copy1(off).wait_recv())

    def add(i, total):
        at = half - 1 - i if backward else i
        sums[at] = total.astype(BF16)
        return total + got[at].astype(F32)

    lax.fori_loop(0, half, add, jnp.zeros(got.shape[1:], F32))
    each(half, lambda off: copy2(off).start())
    give[0, pair] = sums[pair]
    yield
    late = core if not backward else 1 - core
    mine_late = late.astype(F32)
    other_late = 1.0 - mine_late

    def hand_on(off):
        at = slot(off)
        before = give[0, at].astype(F32)
        own = part(core * half + at)
        give[1, at] = (before + other_late * state[own].astype(F32)).astype(BF16)
        copy3(off).start()
        out[own] = (before + mine_late * theirs[part(at)].astype(F32)).astype(BF16)

    def arrive(off):
        copy2(off).wait_recv()
        hand_on(off)

    hand_on(0)
    each(half, arrive)
    yield
    each(half, lambda off: copy3(off).wait_recv(), 0)
    yield
    each(half, lambda off: copy3(off).wait_send(), 0)
    each(half, lambda off: copy2(off).wait_send())
    each(half, lambda off: copy1(off).wait_send())
    copy0().wait_send()
    yield


def layer_kernel(n, *refs):
    sources, refs = refs[:9], refs[9:]
    out, gh, gv, ggate, gw = refs[:5]
    loaded, refs = refs[5:14], refs[14:]
    hidden, weight, conv, values, gate, cot, first, second, rows = loaded
    proj, prev, later, mixed, state, before, grad_state, after = refs[:8]
    dq, dk, dv, gm, gp, hid, gps, part, got = refs[8:17]
    s_ref, num_ref, one_ref, two_ref, ng_ref, inv_ref, gd_ref, norms1, norms2 = refs[17:26]
    scan1, scan2 = refs[26:31], refs[31:36]
    sems1, sems2 = refs[36:44], refs[44:52]
    sh, rh, halo, sa, ra, sb, rb, sc, rc, sd, rd, se, re, load, sn1, rn1, sn2, rn2 = refs[52:]
    tables = (first, second, rows)
    length = hidden.shape[0]

    dp, me = lax.axis_index("dp"), lax.axis_index("ctx")
    count = n // 4
    place, sub = me // 4, lax.rem(me, 4)
    row, core = sub // 2, lax.rem(sub, 2)
    own = dp * 4 + sub
    width = hid.shape[2]

    def peer(off):
        return lax.rem(place + off, count)

    def slot(off):
        return lax.rem(place + count - off, count)

    def far(off):
        return (dp, peer(off) * 4 + sub)

    def side(dx, dy):
        return lax.rem(dp + dx, 2), lax.rem(row + dy, 2) * 2 + core

    def device(dx, dy):
        x, low = side(dx, dy)
        return (x, place * 4 + low)

    def ident(dx, dy):
        x, low = side(dx, dy)
        return x * 4 + low

    other = (dp, place * 4 + row * 2 + 1 - core)
    sides = [(0, 0), (0, 1), (1, 0), (1, 1)]

    def mate(off):
        return lax.rem(own + off, 8)

    def member(i):
        return (i // 4, place * 4 + lax.rem(i, 4))

    def columns(i):
        return pl.ds(pl.multiple_of(i * width, width), width)

    def copy_hid(off):
        return remote(
            hidden.at[:, columns(mate(off))], hid.at[own], sh.at[off], rh.at[off], member(mate(off))
        )

    def copy_prev():
        return remote(proj.at[pl.ds(length - 16, 16)], prev, halo.at[0], halo.at[1], (dp, me + 1))

    def copy_later():
        return remote(gm.at[pl.ds(0, 8)], later, halo.at[2], halo.at[3], (dp, me - 1))

    def copy_gp(r):
        return remote(gp, gps.at[own], sa.at[r], ra.at[r], device(*sides[r]))

    def copy_gp_on(r):
        ref = gps.at[ident(*sides[r])]
        return remote(gp if r == 0 else ref, ref, sb.at[r], rb.at[r], other)

    def copy_part(off):
        return remote(part.at[peer(off)], got.at[place], sc.at[off], rc.at[off], far(off))

    def copy_sum(off):
        ref = gw.at[own, place]
        return remote(ref, ref, sd.at[off], rd.at[off], far(off))

    def copy_on(key, off):
        one, two = ((0, 1), (1, 0)) if off % 2 == 0 else ((1, 0), (0, 1))
        source = ((0, 0), (0, 0), one, (0, 0), one, two, (1, 1))[key]
        target = other if key > 2 else device(*(one if key == 0 else two))
        ref = gw.at[ident(*source), slot(off)]
        return remote(ref, ref, se.at[key, off], re.at[key, off], target)

    def fetch(i):
        return pltpu.make_async_copy(sources[i], loaded[i], load.at[i])

    def copy_norm(ref, s, r, off):
        return remote(ref.at[me], ref.at[me], s.at[off], r.at[off], (dp, lax.rem(me + off, n)))

    def norm_total(ref, after_me):
        def add(i, total):
            use = i > me if after_me else i < me
            return total + jnp.where(use, 1.0, 0.0) * ref[i]

        return lax.fori_loop(0, n, add, jnp.zeros(ref.shape[1:], F32))

    for i in range(9):
        fetch(i).start()
    barrier = pltpu.get_barrier_semaphore()
    each(n, lambda off: greet((dp, lax.rem(me + off, n))))
    each(4, lambda i: greet((1 - dp, place * 4 + i)), 0)
    fetch(0).wait()
    fetch(1).wait()
    proj[...] = mm(hidden[...], weight[...]).astype(BF16)
    pl.semaphore_wait(barrier, n + 3)

    @pl.when(me < n - 1)
    def _():
        copy_prev().start()

    each(8, lambda off: copy_hid(off).start())
    hid[own] = hidden[:, columns(own)]
    for i in range(2, 9):
        fetch(i).wait()

    @pl.when(me > 0)
    def _():
        copy_prev().wait_recv()

    @pl.when(me == 0)
    def _():
        prev[...] = jnp.zeros(prev.shape, BF16)

    mix(proj, prev, conv, mixed)
    norms1[me] = key_part(mixed, values, *tables, state)
    each(n, lambda off: copy_norm(norms1, sn1, rn1, off).start())
    keys_scan = scan_part(n, False, state, before, *scan1, *sems1)
    grad_scan = scan_part(n, True, grad_state, after, *scan2, *sems2)
    next(keys_scan)
    next(keys_scan)
    local_part(mixed, values, *tables, s_ref, num_ref, one_ref, two_ref)
    each(n, lambda off: copy_norm(norms1, sn1, rn1, off).wait_recv())
    norm_in = norm_total(norms1, False)
    next(keys_scan)
    denom_part(norm_in, gate, cot, s_ref, one_ref, two_ref, ng_ref, inv_ref, grad_state)
    next(grad_scan)
    next(keys_scan)
    next(grad_scan)
    next(keys_scan)
    norms2[me] = attend_part(
        gate, cot, before, num_ref, one_ref, two_ref, inv_ref, gd_ref, out, ggate
    )
    each(n, lambda off: copy_norm(norms2, sn2, rn2, off).start())
    next(grad_scan)
    query_part(
        mixed, values, before, norm_in, *tables, s_ref, one_ref, two_ref, ng_ref, gd_ref, dq, dk, dv
    )
    next(grad_scan)
    each(n, lambda off: copy_norm(norms2, sn2, rn2, off).wait_recv())
    norm_after = norm_total(norms2, True)
    next(grad_scan)
    value_part(mixed, values, after, norm_after, dq, dk, dv, *tables, gv, gm)

    @pl.when(me > 0)
    def _():
        copy_later().start()

    @pl.when(me < n - 1)
    def _():
        copy_later().wait_recv()

    @pl.when(me == n - 1)
    def _():
        later[...] = jnp.zeros(later.shape, F32)

    project_back(gm, later, conv, gp)
    for r in range(1, 4):
        copy_gp(r).start()
    copy_gp_on(0).start()
    gps[own] = gp[...]
    gh[...] = mm(gp[...], weight[...], 1, 1).astype(BF16)
    each(8, lambda off: copy_hid(off).wait_recv())
    for r in range(1, 4):
        copy_gp(r).wait_recv()
        copy_gp_on(r).start()
    for r in range(4):
        copy_gp_on(r).wait_recv()
    total = mm(hid[0], gps[0], 0, 0)
    for i in range(1, 8):
        total = total + mm(hid[i], gps[i], 0, 0)
    part[...] = total.reshape(part.shape).astype(BF16)
    each(count, lambda off: copy_part(off).start())
    got[place] = part[place]
    each(count, lambda off: copy_part(off).wait_recv())

    def add(i, total):
        return total + got[i].astype(F32)

    gw[own, place] = lax.fori_loop(0, count, add, jnp.zeros(got.shape[1:], F32)).astype(BF16)
    each(count, lambda off: copy_sum(off).start())
    for step in range(count + 2):
        if step < count:
            if step:
                copy_sum(step).wait_recv()
            for key in (1, 0, 3):
                copy_on(key, step).start()
        if 0 <= step - 1 < count:
            copy_on(0, step - 1).wait_recv()
            copy_on(2, step - 1).start()
            copy_on(4, step - 1).start()
            copy_on(1, step - 1).wait_recv()
            copy_on(5, step - 1).start()
        if step >= 2:
            copy_on(2, step - 2).wait_recv()
            copy_on(6, step - 2).start()
    for off in range(count):
        for key in range(7):
            if key > 2:
                copy_on(key, off).wait_recv()
            copy_on(key, off).wait_send()
    each(count, lambda off: copy_sum(off).wait_send())
    each(count, lambda off: copy_part(off).wait_send())
    for r in range(4):
        if r:
            copy_gp(r).wait_send()
        copy_gp_on(r).wait_send()
    next(keys_scan)
    next(grad_scan)
    each(n, lambda off: copy_norm(norms1, sn1, rn1, off).wait_send())
    each(n, lambda off: copy_norm(norms2, sn2, rn2, off).wait_send())
    each(8, lambda off: copy_hid(off).wait_send())

    @pl.when(me < n - 1)
    def _():
        copy_prev().wait_send()

    @pl.when(me > 0)
    def _():
        copy_later().wait_send()


def write_kernel(*refs):
    copies = [pltpu.make_async_copy(refs[i], refs[5 + i], refs[10].at[i]) for i in range(5)]
    for copy in copies:
        copy.start()
    for copy in copies:
        copy.wait()


def body(n, hidden_in, qk_weight, conv_weight, values, gate_in, cotangent):
    tokens, v, gate, cot = hidden_in[0], values[0], gate_in[0], cotangent[0]
    length, depth = tokens.shape
    cols = qk_weight.shape[1]
    wide = v.shape[1]
    first, second, rows = feature_tables()
    half, count = n // 2, n // 4
    size = 16 * -(-NORM_ROW // (16 * n))
    piece = depth // (8 * count)
    sem, vmem = pltpu.SemaphoreType.DMA, pltpu.VMEM
    state = vmem((n * size, 128), BF16)
    scan = [
        vmem((half * size, 128), BF16), vmem((half * size, 128), BF16),
        vmem((half, size, 128), BF16), vmem((half, size, 128), BF16),
        vmem((2, half, size, 128), BF16),
    ]
    scan_sems = [sem((1,))] * 2 + [sem((half,))] * 6
    outs = [
        ((length, wide), BF16), ((length, depth), BF16), ((length, wide), BF16),
        ((length, wide), BF16), ((8, count, piece, cols), BF16),
    ]
    args = [
        tokens, qk_weight, conv_weight, v, gate, cot,
        jnp.asarray(first, BF16), jnp.asarray(second, BF16), jnp.asarray(rows),
    ]
    results = pl.pallas_call(
        functools.partial(layer_kernel, n),
        out_shape=[jax.ShapeDtypeStruct(s, t) for s, t in outs],
        in_specs=[pl.BlockSpec(memory_space=pl.ANY)] * 9,
        out_specs=[VM] * 5,
        scratch_shapes=[vmem(x.shape, x.dtype) for x in args]
        + [
            vmem((length, cols), BF16), vmem((16, cols), BF16), vmem((8, cols), F32),
            vmem((length, cols), F32), state, state, state, state,
            vmem((length, cols // 2), F32), vmem((length, cols // 2), F32),
            vmem((length, wide), F32), vmem((length, cols), F32), vmem((length, cols), BF16),
            vmem((8, length, depth // 8), BF16), vmem((8, length, cols), BF16),
            vmem((count, piece, cols), BF16), vmem((count, piece, cols), BF16),
            vmem((H, length, length), F32), vmem((H, length, DV), F32),
            vmem((length, H * FP), F32), vmem((length, H * FP), F32),
            vmem((H, length, DV), BF16), vmem((H, length, 1), F32), vmem((H, length, 1), F32),
            vmem((n, 16, 128), F32), vmem((n, 16, 128), F32),
        ]
        + scan * 2 + scan_sems * 2
        + [sem((8,))] * 2 + [sem((4,))] * 5 + [sem((count,))] * 4 + [sem((7, count))] * 2
        + [sem((9,))] + [sem((n,))] * 4,
        compiler_params=pltpu.CompilerParams(
            vmem_limit_bytes=60 * 2**20, collective_id=0, has_side_effects=True
        ),
    )(*args)
    results = list(results)
    results[4] = results[4].reshape(depth, cols)
    out, gh, gv, ggate, gw = pl.pallas_call(
        write_kernel,
        out_shape=[jax.ShapeDtypeStruct(x.shape, x.dtype) for x in results],
        in_specs=[pl.BlockSpec(memory_space=pl.ANY)] * 5,
        out_specs=[pl.BlockSpec(memory_space=pl.ANY)] * 5,
        scratch_shapes=[sem((5,))],
        compiler_params=pltpu.CompilerParams(vmem_limit_bytes=60 * 2**20),
    )(*results)
    return out[None], gh[None], gv[None], ggate[None], gw


def solution(mesh):
    split = P("dp", "ctx", None)
    return jax.shard_map(
        functools.partial(body, mesh.shape["ctx"]),
        mesh=mesh,
        in_specs=(split, P(), P(), split, split, split),
        out_specs=(split, split, split, split, P()),
        check_vma=False,
    )
```

```python
import functools

import jax
import jax.numpy as jnp
import numpy as np
from jax import lax
from jax.experimental import pallas as pl
from jax.experimental.pallas import tpu as pltpu
from jax.sharding import PartitionSpec as P

H = 8
F = 16
DV = 64
KCONV = 3
FP = 256
F32 = jnp.float32
BF16 = jnp.bfloat16
MESH = pl.DeviceIdType.MESH
VM = pl.BlockSpec(memory_space=pltpu.VMEM)
NORM_ROW = H * DV + 2 * DV


def feature_tables():
    pairs = [(a, b) for a in range(F + 1) for b in range(a, F + 1)]
    first = np.zeros((H * F, H * FP), np.float32)
    second = np.zeros((H * F, H * FP), np.float32)
    rows = np.zeros((8, H * FP), np.float32)
    for h in range(H):
        for m, (a, b) in enumerate(pairs):
            lane = h * FP + (m if m < 128 else 128 + 32 * (h % 4) + m - 128)
            if a:
                first[h * F + a - 1, lane] = 1.0
            else:
                rows[0, lane] = 1.0
            if b:
                second[h * F + b - 1, lane] = 1.0
            else:
                rows[1, lane] = 1.0
            scale = 1.0 if b == 0 else 1.0 / F**0.5 if a == 0 else 1.0 / F
            rows[2, lane] = scale * (0.5 if a == b and a else 1.0)
    return first, second, rows


def mm(a, b, ca=1, cb=0):
    return lax.dot_general(a, b, (((ca,), (cb,)), ((), ())), preferred_element_type=F32)


def head_slice(array, h):
    return array[:, h * DV : (h + 1) * DV]


def head_state(state, h):
    tail = H * DV + (h // 4) * DV
    return jnp.concatenate(
        [state[h * DV : (h + 1) * DV], state[tail : tail + DV]], 1
    )


def head_norm(norms, h):
    tail = H + h // 4
    return jnp.concatenate([norms[h : h + 1], norms[tail : tail + 1]], 1)


def store_state(ref, states):
    for h in range(H):
        ref[h * DV : (h + 1) * DV, :] = states[h][:, :128].astype(BF16)
    for g in range(2):
        tail = sum(states[4 * g + i][:, 128:] for i in range(4))
        ref[H * DV + g * DV : H * DV + (g + 1) * DV, :] = tail.astype(BF16)
    rest = ref.shape[0] - NORM_ROW
    if rest:
        ref[NORM_ROW:, :] = jnp.zeros((rest, 128), BF16)


def norm_block(norms):
    rows = [norms[h][:, :128] for h in range(H)]
    rows += [sum(norms[4 * g + i][:, 128:] for i in range(4)) for g in range(2)]
    rows.append(jnp.zeros((16 - len(rows), 128), F32))
    return jnp.concatenate(rows, 0)


def mix(proj, prev, conv, mixed_out):
    length = proj.shape[0]
    padded = jnp.concatenate([prev[8:, :].astype(F32), proj[...].astype(F32)], 0)
    mixed = conv[0:1, :] * padded[8 : 8 + length]
    for j in range(1, KCONV):
        mixed = mixed + conv[j : j + 1, :] * padded[8 - j : 8 - j + length]
    mixed_out[...] = mixed


def key_part(mixed, values, first, second, rows, state_out):
    keys = mixed[:, H * F :].astype(BF16)
    states, norms = [], []
    for h in range(H):
        at = slice(h * FP, (h + 1) * FP)
        phi = (mm(keys, first[:, at]) + rows[0:1, at]) * (mm(keys, second[:, at]) + rows[1:2, at])
        states.append(mm(head_slice(values, h), phi.astype(BF16), 0, 0))
        norms.append(jnp.sum(phi, 0, keepdims=True))
    store_state(state_out, states)
    return norm_block(norms)


def heads_of(mixed):
    lane = lax.broadcasted_iota(jnp.int32, (mixed.shape[0], H * F), 1) // F
    q = mixed[:, : H * F].astype(BF16)
    k = mixed[:, H * F :].astype(BF16)
    zero = jnp.zeros_like(q)
    return q, k, lambda a, h: jnp.where(lane == h, a, zero)


def causal_of(length):
    return lax.broadcasted_iota(jnp.int32, (length, length), 0) >= lax.broadcasted_iota(
        jnp.int32, (length, length), 1
    )


def weights_of(s, causal):
    return jnp.where(causal, 1.0 + s + 0.5 * s * s, 0.0)


def local_part(mixed, values, first, second, rows, s_ref, num_ref, one_ref, two_ref):
    q, k, only = heads_of(mixed)
    causal = causal_of(mixed.shape[0])
    for h in range(H):
        at = slice(h * FP, (h + 1) * FP)
        s = mm(only(q, h), k, 1, 1) * F**-0.5
        s_ref[h] = s
        num_ref[h] = mm(weights_of(s, causal).astype(BF16), head_slice(values, h))
        one_ref[:, at] = mm(q, first[:, at]) + rows[0:1, at]
        two_ref[:, at] = (mm(q, second[:, at]) + rows[1:2, at]) * rows[2:3, at]


def denom_part(norm_rows, gate, cot, s_ref, one_ref, two_ref, ng_ref, inv_ref, state_out):
    causal = causal_of(s_ref.shape[1])
    states = []
    for h in range(H):
        at = slice(h * FP, (h + 1) * FP)
        phi = one_ref[:, at] * two_ref[:, at]
        den = jnp.sum(weights_of(s_ref[h], causal), 1, keepdims=True) + jnp.sum(
            phi * head_norm(norm_rows, h), 1, keepdims=True
        )
        inv = 1.0 / den
        g = head_slice(gate, h).astype(F32)
        ga = head_slice(cot, h).astype(F32) * g / (1.0 + jnp.exp(-g))
        ng = (ga * inv).astype(BF16)
        inv_ref[h] = inv
        ng_ref[h] = ng
        states.append(mm(ng, phi.astype(BF16), 0, 0))
    store_state(state_out, states)


def attend_part(gate, cot, state, num_ref, one_ref, two_ref, inv_ref, gd_ref, out, ggate):
    incoming = state[...]
    norms, outs, ggates = [], [], []
    for h in range(H):
        at = slice(h * FP, (h + 1) * FP)
        phi = one_ref[:, at] * two_ref[:, at]
        inv = inv_ref[h]
        att = (num_ref[h] + mm(phi.astype(BF16), head_state(incoming, h), 1, 1)) * inv
        g = head_slice(gate, h).astype(F32)
        up = head_slice(cot, h).astype(F32)
        sig = 1.0 / (1.0 + jnp.exp(-g))
        act = g * sig
        gd = -jnp.sum(up * act * att, 1, keepdims=True) * inv
        gd_ref[h] = gd
        outs.append((att * act).astype(BF16))
        ggates.append((up * att * sig * (1.0 + g * (1.0 - sig))).astype(BF16))
        norms.append(jnp.sum(gd * phi, 0, keepdims=True))
    for p in range(H // 2):
        at = slice(2 * p * DV, 2 * (p + 1) * DV)
        out[:, at] = jnp.concatenate(outs[2 * p : 2 * p + 2], 1)
        ggate[:, at] = jnp.concatenate(ggates[2 * p : 2 * p + 2], 1)
    return norm_block(norms)


def query_part(
    mixed, values, state, norm_rows, first, second, rows, s_ref, one_ref, two_ref, ng_ref, gd_ref,
    dq_out, dk_out, dv_out,
):
    q, k, only = heads_of(mixed)
    length = mixed.shape[0]
    causal = causal_of(length)
    incoming = state[...]
    dq = jnp.zeros((length, H * F), F32)
    dk = jnp.zeros((length, H * F), F32)
    dvs = []
    for h in range(H):
        at = slice(h * FP, (h + 1) * FP)
        s, ng, gd = s_ref[h], ng_ref[h], gd_ref[h]
        one, two = one_ref[:, at], two_ref[:, at]
        dw = mm(ng, head_slice(values, h), 1, 1) + gd
        ds = (jnp.where(causal, dw * (1.0 + s), 0.0) * F**-0.5).astype(BF16)
        dphi = mm(ng, head_state(incoming, h)) + gd * head_norm(norm_rows, h)
        dq = dq + mm(ds, only(k, h))
        dq = dq + mm((dphi * two).astype(BF16), first[:, at], 1, 1)
        dq = dq + mm((dphi * one * rows[2:3, at]).astype(BF16), second[:, at], 1, 1)
        dk = dk + mm(ds, only(q, h), 0, 0)
        dvs.append(mm(weights_of(s, causal).astype(BF16), ng, 0, 0))
    for p in range(H // 2):
        at = slice(2 * p * DV, 2 * (p + 1) * DV)
        dv_out[:, at] = jnp.concatenate(dvs[2 * p : 2 * p + 2], 1)
    dq_out[...] = dq
    dk_out[...] = dk


def value_part(mixed, values, state, norm_rows, dq_in, dk_in, dv_in, first, second, rows, gv, gm):
    keys = mixed[:, H * F :].astype(BF16)
    incoming = state[...]
    dk = dk_in[...]
    dvs = []
    for h in range(H):
        at = slice(h * FP, (h + 1) * FP)
        first_h, second_h = first[:, at], second[:, at]
        one = mm(keys, first_h) + rows[0:1, at]
        two = mm(keys, second_h) + rows[1:2, at]
        state_h = head_state(incoming, h)
        dphi = mm(head_slice(values, h), state_h) + head_norm(norm_rows, h)
        dk = dk + mm((dphi * two).astype(BF16), first_h, 1, 1)
        dk = dk + mm((dphi * one).astype(BF16), second_h, 1, 1)
        dvs.append(mm((one * two).astype(BF16), state_h, 1, 1))
    for p in range(H // 2):
        at = slice(2 * p * DV, 2 * (p + 1) * DV)
        gv[:, at] = (dv_in[:, at] + jnp.concatenate(dvs[2 * p : 2 * p + 2], 1)).astype(BF16)
    gm[:, : H * F] = dq_in[...]
    gm[:, H * F :] = dk


def project_back(gm, later, conv, gp_out):
    length = gm.shape[0]
    extended = jnp.concatenate([gm[...], later[...]], 0)
    gp = conv[0:1, :] * extended[0:length]
    for j in range(1, KCONV):
        gp = gp + conv[j : j + 1, :] * extended[j : j + length]
    gp_out[...] = gp.astype(BF16)


def remote(src, dst, s, r, device):
    return pltpu.make_async_remote_copy(
        src_ref=src, dst_ref=dst, send_sem=s, recv_sem=r, device_id=device, device_id_type=MESH
    )


def each(count, f, least=1):
    if count <= least:
        return

    def step(off, c):
        f(off)
        return c

    lax.fori_loop(least, count, step, 0)


def greet(device):
    pl.semaphore_signal(
        pltpu.get_barrier_semaphore(), inc=1, device_id=device, device_id_type=MESH
    )


def scan_part(n, backward, state, out, theirs, both, got, sums, give, s0, r0, s1, r1, s2, r2, s3, r3):
    dp, me = lax.axis_index("dp"), lax.axis_index("ctx")
    core, pair = lax.rem(me, 2), me // 2
    half = n // 2
    size = got.shape[1]
    other = (dp, pair * 2 + 1 - core)

    def peer(off):
        return lax.rem(pair + off, half)

    def slot(off):
        return lax.rem(pair + half - off, half)

    def far(off):
        return (dp, peer(off) * 2 + core)

    def part(at, count=1):
        return pl.ds(pl.multiple_of(at * size, 16), count * size)

    def copy0():
        return remote(state.at[part((1 - core) * half, half)], theirs, s0.at[0], r0.at[0], other)

    def copy1(off):
        return remote(both.at[part(peer(off))], got.at[pair], s1.at[off], r1.at[off], far(off))

    def copy2(off):
        return remote(sums.at[peer(off)], give.at[0, pair], s2.at[off], r2.at[off], far(off))

    def copy3(off):
        at = slot(off)
        return remote(
            give.at[1, at], out.at[part(core * half + at)], s3.at[off], r3.at[off], other
        )

    copy0().start()
    yield
    copy0().wait_recv()
    both[...] = (state[part(core * half, half)].astype(F32) + theirs[...].astype(F32)).astype(BF16)
    each(half, lambda off: copy1(off).start())
    got[pair] = both[part(pair)]
    yield
    each(half, lambda off: copy1(off).wait_recv())

    def add(i, total):
        at = half - 1 - i if backward else i
        sums[at] = total.astype(BF16)
        return total + got[at].astype(F32)

    lax.fori_loop(0, half, add, jnp.zeros(got.shape[1:], F32))
    each(half, lambda off: copy2(off).start())
    give[0, pair] = sums[pair]
    yield
    late = core if not backward else 1 - core
    mine_late = late.astype(F32)
    other_late = 1.0 - mine_late

    def hand_on(off):
        at = slot(off)
        before = give[0, at].astype(F32)
        own = part(core * half + at)
        give[1, at] = (before + other_late * state[own].astype(F32)).astype(BF16)
        copy3(off).start()
        out[own] = (before + mine_late * theirs[part(at)].astype(F32)).astype(BF16)

    def arrive(off):
        copy2(off).wait_recv()
        hand_on(off)

    hand_on(0)
    each(half, arrive)
    yield
    each(half, lambda off: copy3(off).wait_recv(), 0)
    yield
    each(half, lambda off: copy3(off).wait_send(), 0)
    each(half, lambda off: copy2(off).wait_send())
    each(half, lambda off: copy1(off).wait_send())
    copy0().wait_send()
    yield


def layer_kernel(n, *refs):
    sources, refs = refs[:9], refs[9:]
    out, gh, gv, ggate, gw = refs[:5]
    loaded, refs = refs[5:14], refs[14:]
    hidden, weight, conv, values, gate, cot, first, second, rows = loaded
    proj, prev, later, mixed, state, before, grad_state, after = refs[:8]
    dq, dk, dv, gm, gp, hid, gps, part, got = refs[8:17]
    s_ref, num_ref, one_ref, two_ref, ng_ref, inv_ref, gd_ref, norms1, norms2 = refs[17:26]
    scan1, scan2 = refs[26:31], refs[31:36]
    sems1, sems2 = refs[36:44], refs[44:52]
    sh, rh, halo, sa, ra, sb, rb, sc, rc, sd, rd, se, re, load, sn1, rn1, sn2, rn2 = refs[52:]
    tables = (first, second, rows)
    length = hidden.shape[0]

    dp, me = lax.axis_index("dp"), lax.axis_index("ctx")
    count = n // 4
    place, sub = me // 4, lax.rem(me, 4)
    row, core = sub // 2, lax.rem(sub, 2)
    own = dp * 4 + sub
    width = hid.shape[2]

    def peer(off):
        return lax.rem(place + off, count)

    def slot(off):
        return lax.rem(place + count - off, count)

    def far(off):
        return (dp, peer(off) * 4 + sub)

    def side(dx, dy):
        return lax.rem(dp + dx, 2), lax.rem(row + dy, 2) * 2 + core

    def device(dx, dy):
        x, low = side(dx, dy)
        return (x, place * 4 + low)

    def ident(dx, dy):
        x, low = side(dx, dy)
        return x * 4 + low

    other = (dp, place * 4 + row * 2 + 1 - core)
    sides = [(0, 0), (0, 1), (1, 0), (1, 1)]

    def mate(off):
        return lax.rem(own + off, 8)

    def member(i):
        return (i // 4, place * 4 + lax.rem(i, 4))

    def columns(i):
        return pl.ds(pl.multiple_of(i * width, width), width)

    def copy_hid(off):
        return remote(
            hidden.at[:, columns(mate(off))], hid.at[own], sh.at[off], rh.at[off], member(mate(off))
        )

    def copy_prev():
        return remote(proj.at[pl.ds(length - 16, 16)], prev, halo.at[0], halo.at[1], (dp, me + 1))

    def copy_later():
        return remote(gm.at[pl.ds(0, 8)], later, halo.at[2], halo.at[3], (dp, me - 1))

    def copy_gp(r):
        return remote(gp, gps.at[own], sa.at[r], ra.at[r], device(*sides[r]))

    def copy_gp_on(r):
        ref = gps.at[ident(*sides[r])]
        return remote(gp if r == 0 else ref, ref, sb.at[r], rb.at[r], other)

    def copy_part(off):
        return remote(part.at[peer(off)], got.at[place], sc.at[off], rc.at[off], far(off))

    def copy_sum(off):
        ref = gw.at[own, place]
        return remote(ref, ref, sd.at[off], rd.at[off], far(off))

    def copy_on(key, off):
        one, two = ((0, 1), (1, 0)) if off % 2 == 0 else ((1, 0), (0, 1))
        source = ((0, 0), (0, 0), one, (0, 0), one, two, (1, 1))[key]
        target = other if key > 2 else device(*(one if key == 0 else two))
        ref = gw.at[ident(*source), slot(off)]
        return remote(ref, ref, se.at[key, off], re.at[key, off], target)

    def fetch(i):
        return pltpu.make_async_copy(sources[i], loaded[i], load.at[i])

    def copy_norm(ref, s, r, off):
        return remote(ref.at[me], ref.at[me], s.at[off], r.at[off], (dp, lax.rem(me + off, n)))

    def norm_total(ref, after_me):
        def add(i, total):
            use = i > me if after_me else i < me
            return total + jnp.where(use, 1.0, 0.0) * ref[i]

        return lax.fori_loop(0, n, add, jnp.zeros(ref.shape[1:], F32))

    for i in range(9):
        fetch(i).start()
    barrier = pltpu.get_barrier_semaphore()
    each(n, lambda off: greet((dp, lax.rem(me + off, n))))
    each(4, lambda i: greet((1 - dp, place * 4 + i)), 0)
    fetch(0).wait()
    fetch(1).wait()
    proj[...] = mm(hidden[...], weight[...]).astype(BF16)
    pl.semaphore_wait(barrier, n + 3)

    @pl.when(me < n - 1)
    def _():
        copy_prev().start()

    hid[own] = hidden[:, columns(own)]
    for i in range(2, 9):
        fetch(i).wait()

    @pl.when(me > 0)
    def _():
        copy_prev().wait_recv()

    @pl.when(me == 0)
    def _():
        prev[...] = jnp.zeros(prev.shape, BF16)

    mix(proj, prev, conv, mixed)
    norms1[me] = key_part(mixed, values, *tables, state)
    each(n, lambda off: copy_norm(norms1, sn1, rn1, off).start())
    copy_hid(1).start()
    keys_scan = scan_part(n, False, state, before, *scan1, *sems1)
    grad_scan = scan_part(n, True, grad_state, after, *scan2, *sems2)
    next(keys_scan)
    next(keys_scan)
    copy_hid(2).start()
    local_part(mixed, values, *tables, s_ref, num_ref, one_ref, two_ref)
    each(n, lambda off: copy_norm(norms1, sn1, rn1, off).wait_recv())
    norm_in = norm_total(norms1, False)
    next(keys_scan)
    copy_hid(3).start()
    denom_part(norm_in, gate, cot, s_ref, one_ref, two_ref, ng_ref, inv_ref, grad_state)
    next(grad_scan)
    next(keys_scan)
    copy_hid(4).start()
    next(grad_scan)
    copy_hid(5).start()
    next(keys_scan)
    norms2[me] = attend_part(
        gate, cot, before, num_ref, one_ref, two_ref, inv_ref, gd_ref, out, ggate
    )
    each(n, lambda off: copy_norm(norms2, sn2, rn2, off).start())
    next(grad_scan)
    copy_hid(6).start()
    copy_hid(7).start()
    query_part(
        mixed, values, before, norm_in, *tables, s_ref, one_ref, two_ref, ng_ref, gd_ref, dq, dk, dv
    )
    next(grad_scan)
    each(n, lambda off: copy_norm(norms2, sn2, rn2, off).wait_recv())
    norm_after = norm_total(norms2, True)
    next(grad_scan)
    value_part(mixed, values, after, norm_after, dq, dk, dv, *tables, gv, gm)

    @pl.when(me > 0)
    def _():
        copy_later().start()

    @pl.when(me < n - 1)
    def _():
        copy_later().wait_recv()

    @pl.when(me == n - 1)
    def _():
        later[...] = jnp.zeros(later.shape, F32)

    project_back(gm, later, conv, gp)
    for r in range(1, 4):
        copy_gp(r).start()
    copy_gp_on(0).start()
    gps[own] = gp[...]
    gh[...] = mm(gp[...], weight[...], 1, 1).astype(BF16)
    each(8, lambda off: copy_hid(off).wait_recv())
    for r in range(1, 4):
        copy_gp(r).wait_recv()
        copy_gp_on(r).start()
    for r in range(4):
        copy_gp_on(r).wait_recv()
    total = mm(hid[0], gps[0], 0, 0)
    for i in range(1, 8):
        total = total + mm(hid[i], gps[i], 0, 0)
    part[...] = total.reshape(part.shape).astype(BF16)
    each(count, lambda off: copy_part(off).start())
    got[place] = part[place]
    each(count, lambda off: copy_part(off).wait_recv())

    def add(i, total):
        return total + got[i].astype(F32)

    gw[own, place] = lax.fori_loop(0, count, add, jnp.zeros(got.shape[1:], F32)).astype(BF16)
    each(count, lambda off: copy_sum(off).start())
    for step in range(count + 2):
        if step < count:
            if step:
                copy_sum(step).wait_recv()
            for key in (1, 0, 3):
                copy_on(key, step).start()
        if 0 <= step - 1 < count:
            copy_on(0, step - 1).wait_recv()
            copy_on(2, step - 1).start()
            copy_on(4, step - 1).start()
            copy_on(1, step - 1).wait_recv()
            copy_on(5, step - 1).start()
        if step >= 2:
            copy_on(2, step - 2).wait_recv()
            copy_on(6, step - 2).start()
    for off in range(count):
        for key in range(7):
            if key > 2:
                copy_on(key, off).wait_recv()
            copy_on(key, off).wait_send()
    each(count, lambda off: copy_sum(off).wait_send())
    each(count, lambda off: copy_part(off).wait_send())
    for r in range(4):
        if r:
            copy_gp(r).wait_send()
        copy_gp_on(r).wait_send()
    next(keys_scan)
    next(grad_scan)
    each(n, lambda off: copy_norm(norms1, sn1, rn1, off).wait_send())
    each(n, lambda off: copy_norm(norms2, sn2, rn2, off).wait_send())
    each(8, lambda off: copy_hid(off).wait_send())

    @pl.when(me < n - 1)
    def _():
        copy_prev().wait_send()

    @pl.when(me > 0)
    def _():
        copy_later().wait_send()


def write_kernel(*refs):
    sources, outs, held, loads, stores = refs[:5], refs[5:10], refs[10:15], refs[15], refs[16]
    reads = [pltpu.make_async_copy(sources[i], held[i], loads.at[i]) for i in range(5)]
    writes = [pltpu.make_async_copy(held[i], outs[i], stores.at[i]) for i in range(5)]
    for read in reads:
        read.start()
    for read, write in zip(reads, writes):
        read.wait()
        write.start()
    for write in writes:
        write.wait()


def body(n, hidden_in, qk_weight, conv_weight, values, gate_in, cotangent):
    tokens, v, gate, cot = hidden_in[0], values[0], gate_in[0], cotangent[0]
    length, depth = tokens.shape
    cols = qk_weight.shape[1]
    wide = v.shape[1]
    first, second, rows = feature_tables()
    half, count = n // 2, n // 4
    size = 16 * -(-NORM_ROW // (16 * n))
    piece = depth // (8 * count)
    sem, vmem = pltpu.SemaphoreType.DMA, pltpu.VMEM
    state = vmem((n * size, 128), BF16)
    scan = [
        vmem((half * size, 128), BF16), vmem((half * size, 128), BF16),
        vmem((half, size, 128), BF16), vmem((half, size, 128), BF16),
        vmem((2, half, size, 128), BF16),
    ]
    scan_sems = [sem((1,))] * 2 + [sem((half,))] * 6
    outs = [
        ((length, wide), BF16), ((length, depth), BF16), ((length, wide), BF16),
        ((length, wide), BF16), ((8, count, piece, cols), BF16),
    ]
    args = [
        tokens, qk_weight, conv_weight, v, gate, cot,
        jnp.asarray(first, BF16), jnp.asarray(second, BF16), jnp.asarray(rows),
    ]
    results = pl.pallas_call(
        functools.partial(layer_kernel, n),
        out_shape=[jax.ShapeDtypeStruct(s, t) for s, t in outs],
        in_specs=[pl.BlockSpec(memory_space=pl.ANY)] * 9,
        out_specs=[VM] * 5,
        scratch_shapes=[vmem(x.shape, x.dtype) for x in args]
        + [
            vmem((length, cols), BF16), vmem((16, cols), BF16), vmem((8, cols), F32),
            vmem((length, cols), F32), state, state, state, state,
            vmem((length, cols // 2), F32), vmem((length, cols // 2), F32),
            vmem((length, wide), F32), vmem((length, cols), F32), vmem((length, cols), BF16),
            vmem((8, length, depth // 8), BF16), vmem((8, length, cols), BF16),
            vmem((count, piece, cols), BF16), vmem((count, piece, cols), BF16),
            vmem((H, length, length), F32), vmem((H, length, DV), F32),
            vmem((length, H * FP), F32), vmem((length, H * FP), F32),
            vmem((H, length, DV), BF16), vmem((H, length, 1), F32), vmem((H, length, 1), F32),
            vmem((n, 16, 128), F32), vmem((n, 16, 128), F32),
        ]
        + scan * 2 + scan_sems * 2
        + [sem((8,))] * 2 + [sem((4,))] * 5 + [sem((count,))] * 4 + [sem((7, count))] * 2
        + [sem((9,))] + [sem((n,))] * 4,
        compiler_params=pltpu.CompilerParams(
            vmem_limit_bytes=60 * 2**20, collective_id=0, has_side_effects=True
        ),
    )(*args)
    results = list(results)
    results[4] = results[4].reshape(depth, cols)
    out, gh, gv, ggate, gw = pl.pallas_call(
        write_kernel,
        out_shape=[jax.ShapeDtypeStruct(x.shape, x.dtype) for x in results],
        in_specs=[pl.BlockSpec(memory_space=pl.ANY)] * 5,
        out_specs=[pl.BlockSpec(memory_space=pl.ANY)] * 5,
        scratch_shapes=[vmem(x.shape, x.dtype) for x in results] + [sem((5,))] * 2,
        compiler_params=pltpu.CompilerParams(vmem_limit_bytes=60 * 2**20),
    )(*results)
    return out[None], gh[None], gv[None], ggate[None], gw


def solution(mesh):
    split = P("dp", "ctx", None)
    return jax.shard_map(
        functools.partial(body, mesh.shape["ctx"]),
        mesh=mesh,
        in_specs=(split, P(), P(), split, split, split),
        out_specs=(split, split, split, split, P()),
        check_vma=False,
    )
```
